256 devices in a mesh: group: 8 (over y, core), worker: 32 (over x, z).
Axes of the slice: x: 4, y: 4, z: 8, core: 2. Of those that a mesh axis runs over, the one named last changes fastest.
Arguments:
- green_tensor: bfloat16 [4096, 1024], P(('group', 'worker')), may hold values from -0.09375 to 0.09375
- slip_field: float32 [4096, 256], P(('group', 'worker')), may hold values from 0.1 to 3
- rupture_time: float32 [4096, 256], P(('group', 'worker')), may hold values from 0 to 40
- periods: float32 [256], replicated, may hold values from 1 to 10
- owner_map: int32 [256, 1], replicated, may hold values from 0 to 31; in each aligned block of 32 rows (0 to 31, 32 to 63, ...) at most 3 rows name the same one
Outputs:
- spectra_slots: float32 [768, 512], P(('group', 'worker'))
The draws below stay inside these ranges and needn't reach their ends.
Inputs may be any that keep to these rules, and one draw needn't show every extreme that they name: `owner_map`: in each aligned block of 1 * 32 rows (one group's variations) no worker is named by more than 3 rows; in some block one worker is named by exactly 3.
All inputs are finite; a program needn't handle non-finite values.
Results may differ from the reference program's by a relative error of at most 0.0024.
Values sent between devices are 32-bit elements; how exact they have to be, the bound alone decides.
A program may use at most 64 MiB of HBM per device.

```python
import math
import jax
import jax.numpy as jnp
import numpy as np
from jax import lax

NT = 4096
NF = 256
NP = 256
V_DEV = 1
MOST = 3
S = 4096
V = 256
SLOTS = 768
N_GROUP = 8
N_WORKER = 32


def shard_levels(key, shape, split, low, top_value):
    gain, own = 1.0, jax.random.fold_in(key, 6)
    for dim, blocks in split:
        steps = jnp.exp(jax.random.uniform(jax.random.fold_in(own, dim), (blocks,), jnp.float32, low / len(split), top_value / len(split)))
        gain = gain * jnp.repeat(steps, shape[dim] // blocks).reshape([-1 if axis == dim else 1 for axis in range(len(shape))])
    return gain


def assign_block(rng, own, number, rows, amount, top, reach, skew):
    order = jax.random.permutation(rng, amount)
    packed, usual = shares(amount, rows * top, reach, skew, True), shares(amount, rows * top, reach, skew, False)
    places = jnp.arange(amount)

    def named(lengths, offset_by):
        used = int((lengths > 0).sum())
        fixed = max(1, used // 4)
        moved = fixed + (places - fixed + offset_by * (used - fixed)) % max(1, amount - fixed)
        return jnp.zeros((amount,), jnp.int32).at[order[jnp.where(places < fixed, places, moved)]].set(jnp.asarray(lengths, jnp.int32))

    lengths = jnp.where(number % 4 == 0, named(packed, number // 4), named(usual, number - number // 4 - 1))
    mixed = jax.random.permutation(jax.random.fold_in(own, 3), amount)
    giver, receiver = mixed[0:amount // 2 * 2:2], mixed[1:amount // 2 * 2:2]
    room = jnp.minimum(lengths[giver] - 1, reach - lengths[receiver]) // 2
    room = jnp.where((giver == order[0]) | (receiver == order[0]) | (lengths[receiver] == 0), 0, jnp.maximum(room, 0))
    moved = jax.random.randint(jax.random.fold_in(own, 4), (amount // 2,), 0, 1 << 20) % (room + 1)
    lengths = lengths.at[giver].add(-moved).at[receiver].add(moved)
    items = jnp.searchsorted(jnp.cumsum(lengths), jnp.arange(rows * top), side="right").astype(jnp.int32)
    grid = items.reshape(top, rows).T
    grid = grid[jax.random.permutation(jax.random.fold_in(own, 1), rows)]
    offset_by = jax.random.randint(jax.random.fold_in(own, 2), (rows, 1), 0, top)
    return jnp.take_along_axis(grid, (jnp.arange(top)[None, :] + offset_by) % top, axis=1)


def shares(count, total, reach, lean, full):
    weights = [(1 << 20) // math.isqrt(grade ** lean) + 1 for grade in range(1, count + 1)]
    largest = reach if full else min(reach, max(-(-total // count), total * weights[0] // sum(weights)))
    least = 1 if total - largest >= count - 1 else 0
    counts, spare = [largest] + [least] * (count - 1), total - largest - least * (count - 1)
    while spare > 0:
        free = [i for i in range(1, count) if counts[i] < largest] or [i for i in range(1, count) if counts[i] < reach]
        whole, left = sum([weights[i] for i in free]), spare
        for i in free:
            more = min(reach - counts[i], max(1, left * weights[i] // whole), spare)
            counts[i] = counts[i] + more
            spare = spare - more
    return np.array(counts)


def bell_draw(key, extent, width, bound, split=(), kind=jnp.bfloat16):
    gain = shard_levels(key, extent, split, -0.22, 0.18) if split else 1.0
    entries = jax.random.normal(key, extent, jnp.float32) * width * gain
    return jnp.minimum(jnp.maximum(entries, -bound), bound).astype(kind)


def setup_inputs(seed: int = 0) -> dict:
    splits = jax.random.split(jax.random.key(seed), 6)
    green_tensor = bell_draw(splits[0], (S, 4 * NF), S ** -0.5, 0.09375, ((0, 256),))
    slip_field = jnp.clip(jnp.exp(math.log(3.0) - 3.4011974 * jax.random.uniform(splits[1], (S, V), jnp.float32) ** shard_levels(splits[1], (S, V), ((0, 256),), -0.2, 0.2)), 0.1, 3.0)
    rupture_time = jnp.clip(40.0 * jax.random.uniform(splits[2], (S, V), jnp.float32) ** shard_levels(splits[2], (S, V), ((0, 256),), -0.2, 0.2), 0.0, 40.0)
    periods = jnp.clip(jnp.exp(jax.random.uniform(splits[3], (NP,), jnp.float32, math.log(1.0), math.log(10.0))), 1.0, 10.0)
    owner_map_keys = jax.random.split(jax.random.fold_in(splits[4], 1), V // (V_DEV * N_WORKER))
    owner_map_turns = jax.random.permutation(jax.random.fold_in(splits[4], 3), V // (V_DEV * N_WORKER))
    owner_map = jax.vmap(lambda own, number: assign_block(jax.random.fold_in(splits[4], 2), own, number, V_DEV * N_WORKER, N_WORKER, 1, MOST, 2))(owner_map_keys, owner_map_turns).reshape((V, 1))
    return {"green_tensor": green_tensor, "slip_field": slip_field, "rupture_time": rupture_time, "periods": periods, "owner_map": owner_map}


time_step = 0.05
damping = 0.05

def angular_grid():
    return 2.0 * math.pi * jnp.arange(NF, dtype=jnp.float32) / (NT * time_step)

def oscillator_gains(periods):
    natural = 2.0 * math.pi / periods
    angular = angular_grid()
    denom_real = natural[:, None] ** 2 - angular[None, :] ** 2
    denom_imag = 2.0 * damping * natural[:, None] * angular[None, :]
    modulus = denom_real ** 2 + denom_imag ** 2
    scale = natural[:, None] ** 2 / modulus
    return (-scale * denom_real, scale * denom_imag)

def basis_table():
    freq_index = jnp.arange(NF, dtype=jnp.int32)
    time_index = jnp.arange(NT, dtype=jnp.int32)
    turns = freq_index[:, None] * time_index[None, :] % NT
    angle_grid = 2.0 * math.pi / NT * turns.astype(jnp.float32)
    fold_weight = jnp.where(freq_index == 0, 1.0, 2.0).astype(jnp.float32)[:, None]
    return jnp.concatenate([fold_weight * jnp.cos(angle_grid), -fold_weight * jnp.sin(angle_grid)], 0).astype(jnp.bfloat16)

def slot_selector(owner_map):
    owners = owner_map[:, 0].reshape(N_GROUP, V_DEV * N_WORKER)
    matches = (owners[:, :, None] == jnp.arange(N_WORKER, dtype=jnp.int32)[None, None, :]).astype(jnp.int32)
    ranking = jnp.cumsum(matches, axis=1) - 1
    slot_index = lax.optimization_barrier(jnp.sum(matches * ranking, axis=2))
    hits = owners[:, None, None, :] == jnp.arange(N_WORKER, dtype=jnp.int32)[None, :, None, None]
    hits = hits & (slot_index[:, None, None, :] == jnp.arange(MOST, dtype=jnp.int32)[None, None, :, None])
    return hits.astype(jnp.float32)

def reference(green_tensor, slip_field, rupture_time, periods, owner_map):
    angular = angular_grid()
    green = green_tensor.astype(jnp.float32).reshape(S, 2, 2, NF)
    high = lax.Precision.HIGHEST

    def one_freq(freq):
        phase = angular[freq] * rupture_time
        cos_part = (slip_field * jnp.cos(phase)).astype(jnp.bfloat16).astype(jnp.float32)
        sin_part = (slip_field * jnp.sin(phase)).astype(jnp.bfloat16).astype(jnp.float32)
        green_real = green[:, :, 0, freq]
        green_imag = green[:, :, 1, freq]
        real_part = jnp.dot(cos_part.T, green_real, precision=high) + jnp.dot(sin_part.T, green_imag, precision=high)
        imag_part = jnp.dot(cos_part.T, green_imag, precision=high) - jnp.dot(sin_part.T, green_real, precision=high)
        return jnp.stack([real_part, imag_part], axis=2)
    spectrum = lax.map(one_freq, jnp.arange(NF, dtype=jnp.int32))
    spectrum = jnp.transpose(spectrum, (1, 2, 3, 0))
    gain_real, gain_imag = oscillator_gains(periods)
    basis = basis_table().astype(jnp.float32)

    def peaks(single):
        spec_real = single[:, 0][:, None, :]
        spec_imag = single[:, 1][:, None, :]
        weighted_real = spec_real * gain_real - spec_imag * gain_imag
        weighted_imag = spec_real * gain_imag + spec_imag * gain_real
        weighted = jnp.concatenate([weighted_real, weighted_imag], -1).astype(jnp.bfloat16)
        weighted = weighted.reshape(2 * NP, 2 * NF).astype(jnp.float32)
        response = jnp.dot(weighted, basis, precision=high)
        return lax.optimization_barrier(jnp.max(jnp.abs(response), axis=1)) / math.sqrt(NF)
    peak_all = lax.map(peaks, spectrum)
    selector = slot_selector(owner_map)
    grouped = peak_all.reshape(N_GROUP, V_DEV * N_WORKER, 2 * NP)
    placed = jnp.einsum('gojv,gvx->gojx', selector, grouped, precision=high)
    return placed.reshape(SLOTS, 2 * NP)
```

```python
import functools
import math

import jax
import jax.numpy as jnp
from jax import lax
from jax.experimental import pallas as pl
from jax.experimental.pallas import tpu as pltpu
from jax.sharding import PartitionSpec as P

NT = 4096
NF = 256
NP = 256
MOST = 3
TIME_STEP = 0.05
DAMPING = 0.05

GROUPS = 8
WORKERS = 32
ROWS = 16
GATHERED = ROWS * GROUPS
HALF = 128
STEPS = 64
TIMES = NT // 2 + 16

f32 = jnp.float32
bf16 = jnp.bfloat16
MESH = pl.DeviceIdType.MESH


def cos_sin_turns(turns):
    near = turns - jnp.round(turns)
    angle = near * (2.0 * math.pi)
    square = angle * angle
    cos = f32(0.0)
    for n in range(8, -1, -1):
        cos = cos * square + f32((-1) ** n / math.factorial(2 * n))
    sin = f32(0.0)
    for n in range(8, -1, -1):
        sin = sin * square + f32((-1) ** n / math.factorial(2 * n + 1))
    return cos, sin * angle


def kernel(
    green_ref, slip_ref, time_ref, periods_ref, owner_ref, out_ref,
    basis, green_stage, field_stage, green_all, field_all, phasors, lhs, spectra,
    partial, arrived, halves, peaks, gain, chosen,
    field_send, field_recv, green_send, green_recv,
    sum_send, sum_recv, half_send, half_recv, peak_send, peak_recv,
):
    group = lax.axis_index("group")
    worker = lax.axis_index("worker")
    row, core = group // 2, group % 2

    barrier = pltpu.get_barrier_semaphore()
    for i in range(1, GROUPS):
        pl.semaphore_signal(
            barrier, inc=1, device_id={"group": (group + i) % GROUPS}, device_id_type=MESH
        )
    for i in range(1, WORKERS):
        pl.semaphore_signal(
            barrier, inc=1, device_id={"worker": (worker + i) % WORKERS}, device_id_type=MESH
        )

    with jax.named_scope("stage"):
        for y in range(GROUPS // 2):
            lanes = slice(64 * y, 64 * y + 64)
            field_stage[y] = jnp.concatenate([slip_ref[:, lanes], time_ref[:, lanes]], axis=1)
        for c in range(2):
            for part in range(4):
                start = part * NF + c * HALF
                green_stage[c, :, part * HALF : (part + 1) * HALF] = green_ref[
                    :, start : start + HALF
                ].astype(f32)

    with jax.named_scope("barrier"):
        pl.semaphore_wait(barrier, GROUPS - 1 + WORKERS - 1)

    mine = pl.ds(pl.multiple_of(ROWS * group, ROWS), ROWS)
    sent = []
    with jax.named_scope("send_fields"):
        for i in range(1, GROUPS):
            to = (group + i) % GROUPS
            copy = pltpu.make_async_remote_copy(
                src_ref=field_stage.at[to // 2],
                dst_ref=field_all.at[mine],
                send_sem=field_send,
                recv_sem=field_recv,
                device_id={"group": to},
                device_id_type=MESH,
            )
            copy.start()
        for i in range(1, GROUPS):
            to = (group + i) % GROUPS
            copy = pltpu.make_async_remote_copy(
                src_ref=green_stage.at[to % 2],
                dst_ref=green_all.at[mine],
                send_sem=green_send,
                recv_sem=green_recv,
                device_id={"group": to},
                device_id_type=MESH,
            )
            copy.start()
    field_all[mine, :] = field_stage[row]
    green_all[mine, :] = green_stage[core]

    with jax.named_scope("gain"):
        natural = (2.0 * math.pi) / periods_ref[...]
        column = jnp.concatenate(
            [
                jnp.transpose(jnp.broadcast_to(natural[:, :128], (128, 128))),
                jnp.transpose(jnp.broadcast_to(natural[:, 128:], (128, 128))),
            ],
            axis=0,
        )
        for h in range(2):
            index = lax.broadcasted_iota(jnp.int32, (NP, 128), 1) + 128 * h
            angular = (2.0 * math.pi) * index.astype(f32) / (NT * TIME_STEP)
            denom_real = column * column - angular * angular
            denom_imag = (2.0 * DAMPING) * column * angular
            scale = column * column / (denom_real * denom_real + denom_imag * denom_imag)
            gain[0, :, 128 * h : 128 * h + 128] = -scale * denom_real
            gain[1, :, 128 * h : 128 * h + 128] = scale * denom_imag

    with jax.named_scope("basis"):
        freq = lax.broadcasted_iota(jnp.int32, (16, NF), 1)
        time = lax.broadcasted_iota(jnp.int32, (16, NF), 0)
        fold = jnp.where(freq == 0, 1.0, 2.0)
        cos0, sin0 = cos_sin_turns((freq * time).astype(f32) * (1.0 / NT))
        cos16, sin16 = cos_sin_turns(freq.astype(f32) * (16.0 / NT))

        def advance(b, carry):
            cos, sin = carry
            rows = pl.ds(pl.multiple_of(16 * b, 16), 16)
            basis[0, rows, :] = cos.astype(bf16)
            basis[1, rows, :] = sin.astype(bf16)
            return cos * cos16 + sin * sin16, sin * cos16 - cos * sin16

        lax.fori_loop(0, TIMES // 16, advance, (fold * cos0, -fold * sin0), unroll=3)

    with jax.named_scope("owners"):
        count = jnp.int32(0)
        for i in range(WORKERS):
            hit = (owner_ref[WORKERS * group + i] == worker).astype(jnp.int32)
            for j in range(MOST):
                value = (hit * (count == j).astype(jnp.int32)).astype(f32)
                chosen[j, i] = jnp.full((4, 128), value, f32)
            count = count + hit

    with jax.named_scope("wait_fields"):
        others = pl.ds(0, ROWS * (GROUPS - 1))
        pltpu.make_async_copy(field_all.at[others], field_all.at[others], field_recv).wait()

    with jax.named_scope("phasors"):
        for s in range(0, GATHERED, 32):
            field = field_all[s : s + 32, :]
            swapped = pltpu.roll(field, 64, 1)
            lane = lax.broadcasted_iota(jnp.int32, (32, 128), 1)
            low = lane < 64
            slip = jnp.where(low, field, swapped)
            turn = jnp.where(low, swapped, field) * (1.0 / (NT * TIME_STEP))
            first = (core * HALF + jnp.where(low, 0, STEPS)).astype(f32)
            cos0, sin0 = cos_sin_turns(turn * first)
            cos1, sin1 = cos_sin_turns(turn)

            def step(k, carry, s=s, cos1=cos1, sin1=sin1):
                cos, sin = carry
                phasors[k, s : s + 32, :] = cos.astype(bf16)
                phasors[k, GATHERED + s : GATHERED + s + 32, :] = sin.astype(bf16)
                return cos * cos1 - sin * sin1, sin * cos1 + cos * sin1

            lax.fori_loop(0, STEPS, step, (slip * cos0, slip * sin0), unroll=8)

    with jax.named_scope("wait_green"):
        pltpu.make_async_copy(green_all.at[others], green_all.at[others], green_recv).wait()

    with jax.named_scope("green"):
        for c in range(2):
            for part in range(2):
                at = (2 * c + part) * HALF
                turned = jnp.transpose(green_all[:, at : at + HALF])
                for h in range(2):
                    value = turned[STEPS * h : STEPS * h + STEPS, :]
                    real = pl.ds(4 * h + 2 * c, STEPS, stride=8)
                    imag = pl.ds(4 * h + 2 * c + 1, STEPS, stride=8)
                    if part == 0:
                        lhs[0, real, :] = value
                        lhs[1, imag, :] = -value
                    else:
                        lhs[1, real, :] = value
                        lhs[0, imag, :] = value

    with jax.named_scope("spectra"):

        def product(k, _):
            rows = pl.ds(pl.multiple_of(8 * k, 8), 8)
            spectra[rows, :] = jnp.dot(
                jnp.concatenate([lhs[0, rows, :], lhs[1, rows, :]], axis=1).astype(bf16),
                phasors[k],
                preferred_element_type=f32,
            )
            return 0

        lax.fori_loop(0, STEPS, product, 0, unroll=8)

    with jax.named_scope("turn"):
        low = lax.broadcasted_iota(jnp.int32, (64, 128), 1) < 64
        for r in range(4):
            both = jnp.concatenate(
                [spectra[pl.ds(r, STEPS, stride=8), :], spectra[pl.ds(4 + r, STEPS, stride=8), :]],
                axis=0,
            )
            turned = jnp.transpose(both)
            value = jnp.where(low, turned[:64], turned[64:])
            for c in range(2):
                partial[pl.ds(4 * c + r, WORKERS, stride=8), :] = value[
                    WORKERS * c : WORKERS * c + WORKERS
                ]

    with jax.named_scope("send_sums"):
        for i in range(1, WORKERS):
            to = (worker + i) % WORKERS
            copy = pltpu.make_async_remote_copy(
                src_ref=partial.at[pl.ds(pl.multiple_of(8 * to, 8), 8)],
                dst_ref=arrived.at[worker],
                send_sem=sum_send,
                recv_sem=sum_recv,
                device_id={"worker": to},
                device_id_type=MESH,
            )
            copy.start()
        arrived[worker] = partial[pl.ds(pl.multiple_of(8 * worker, 8), 8), :]
    with jax.named_scope("wait_sums"):
        most = pl.ds(0, WORKERS - 1)
        pltpu.make_async_copy(arrived.at[most], arrived.at[most], sum_recv).wait()

    with jax.named_scope("half"):
        total = arrived[0]
        for i in range(1, WORKERS):
            total = total + arrived[i]
        halves[core] = total
        copy = pltpu.make_async_remote_copy(
            src_ref=halves.at[core],
            dst_ref=halves.at[core],
            send_sem=half_send,
            recv_sem=half_recv,
            device_id={"group": row * 2 + (1 - core)},
            device_id_type=MESH,
        )
        copy.start()
        copy.wait()

    with jax.named_scope("weigh"):
        real, imag = [], []
        for c in range(2):
            for h in range(2):
                spec_real = halves[h, pl.ds(4 * core + 2 * c, 1), :]
                spec_imag = halves[h, pl.ds(4 * core + 2 * c + 1, 1), :]
                gain_real = gain[0, :, 128 * h : 128 * h + 128]
                gain_imag = gain[1, :, 128 * h : 128 * h + 128]
                real.append((spec_real * gain_real - spec_imag * gain_imag).astype(bf16))
                imag.append((spec_real * gain_imag + spec_imag * gain_real).astype(bf16))
        weighted = [
            jnp.concatenate(
                [
                    jnp.concatenate([x[0], x[1]], axis=1),
                    jnp.concatenate([x[2], x[3]], axis=1),
                ],
                axis=0,
            )
            for x in (real, imag)
        ]

    with jax.named_scope("response"):
        contract = (((1,), (1,)), ((), ()))
        best = jnp.zeros((8, 2 * NP), f32)
        for start, size in [(256 * b, 256) for b in range(NT // 512)] + [(NT // 2, 16)]:
            even = lax.dot_general(
                basis[0, start : start + size, :], weighted[0], contract, preferred_element_type=f32
            )
            odd = lax.dot_general(
                basis[1, start : start + size, :], weighted[1], contract, preferred_element_type=f32
            )
            value = jnp.abs(even) + jnp.abs(odd)
            for t in range(0, size, 8):
                best = jnp.maximum(best, value[t : t + 8])
        top = jnp.max(best, axis=0, keepdims=True) * (1.0 / math.sqrt(NF))
        for r in range(4):
            peaks[worker, r : r + 1, :] = top[:, 128 * r : 128 * r + 128]

    with jax.named_scope("send_peaks"):
        for i in range(1, WORKERS):
            copy = pltpu.make_async_remote_copy(
                src_ref=peaks.at[worker],
                dst_ref=peaks.at[worker],
                send_sem=peak_send,
                recv_sem=peak_recv,
                device_id={"worker": (worker + i) % WORKERS},
                device_id_type=MESH,
            )
            copy.start()
    with jax.named_scope("wait_peaks"):
        pltpu.make_async_copy(peaks.at[most], peaks.at[most], peak_recv).wait()

    with jax.named_scope("place"):
        for j in range(MOST):
            total = chosen[j, 0] * peaks[0]
            for i in range(1, WORKERS):
                total = total + chosen[j, i] * peaks[i]
            for r in range(4):
                out_ref[j : j + 1, 128 * r : 128 * r + 128] = total[r : r + 1, :]

    with jax.named_scope("wait_sent"):
        pltpu.make_async_copy(field_all.at[others], field_all.at[others], field_send).wait()
        pltpu.make_async_copy(green_all.at[others], green_all.at[others], green_send).wait()
        pltpu.make_async_copy(arrived.at[most], arrived.at[most], sum_send).wait()
        pltpu.make_async_copy(peaks.at[most], peaks.at[most], peak_send).wait()


def local(green_tensor, slip_field, rupture_time, periods, owner_map):
    vmem = pl.BlockSpec(memory_space=pltpu.VMEM)
    dma = pltpu.SemaphoreType.DMA
    return pl.pallas_call(
        kernel,
        out_shape=jax.ShapeDtypeStruct((MOST, 2 * NP), f32),
        in_specs=[
            vmem,
            vmem,
            vmem,
            vmem,
            pl.BlockSpec(memory_space=pltpu.SMEM),
        ],
        out_specs=vmem,
        scratch_shapes=[
            pltpu.VMEM((2, TIMES, NF), bf16),
            pltpu.VMEM((2, ROWS, 4 * HALF), f32),
            pltpu.VMEM((GROUPS // 2, ROWS, 128), f32),
            pltpu.VMEM((GATHERED, 4 * HALF), f32),
            pltpu.VMEM((GATHERED, 128), f32),
            pltpu.VMEM((STEPS, 2 * GATHERED, 128), bf16),
            pltpu.VMEM((2, 8 * STEPS, GATHERED), f32),
            pltpu.VMEM((8 * STEPS, 128), f32),
            pltpu.VMEM((8 * WORKERS, 128), f32),
            pltpu.VMEM((WORKERS, 8, 128), f32),
            pltpu.VMEM((2, 8, 128), f32),
            pltpu.VMEM((WORKERS, 4, 128), f32),
            pltpu.VMEM((2, NP, NF), f32),
            pltpu.VMEM((MOST, WORKERS, 4, 128), f32),
        ]
        + [dma] * 10,
        compiler_params=pltpu.CompilerParams(
            collective_id=0, has_side_effects=True, vmem_limit_bytes=32 * 1024 * 1024
        ),
        name="seismogram",
    )(
        green_tensor,
        slip_field,
        rupture_time,
        periods.reshape(1, NP),
        owner_map.reshape(-1),
    )


def solution(mesh):
    placed = (
        P(("group", "worker"), None),
        P(("group", "worker"), None),
        P(("group", "worker"), None),
        P(),
        P(),
    )
    return jax.shard_map(
        local, mesh=mesh, in_specs=placed, out_specs=P(("group", "worker"), None), check_vma=False
    )
```

```python
import functools
import math

import jax
import jax.numpy as jnp
from jax import lax
from jax.experimental import pallas as pl
from jax.experimental.pallas import tpu as pltpu
from jax.sharding import PartitionSpec as P

NT = 4096
NF = 256
NP = 256
MOST = 3
TIME_STEP = 0.05
DAMPING = 0.05

GROUPS = 8
WORKERS = 32
LINE = 8
ROWS = 16
STEPS_TO = sorted(
    [(i // LINE, i % LINE) for i in range(1, WORKERS)],
    key=lambda step: -min(step[0], 4 - step[0]) - min(step[1], LINE - step[1]),
)
GATHERED = ROWS * GROUPS
HALF = 128
STEPS = 64
TIMES = NT // 2 + 16

f32 = jnp.float32
bf16 = jnp.bfloat16
MESH = pl.DeviceIdType.MESH


def cos_sin_turns(turns):
    near = turns - jnp.round(turns)
    angle = near * (2.0 * math.pi)
    square = angle * angle
    cos = f32(0.0)
    for n in range(8, -1, -1):
        cos = cos * square + f32((-1) ** n / math.factorial(2 * n))
    sin = f32(0.0)
    for n in range(8, -1, -1):
        sin = sin * square + f32((-1) ** n / math.factorial(2 * n + 1))
    return cos, sin * angle


def kernel(
    green_hbm, slip_hbm, time_hbm, periods_hbm, owner_hbm, out_ref,
    green_ref, slip_ref, time_ref, periods_ref, owner_ref, basis, green_stage, field_stage, green_all, field_all, phasors, lhs, spectra,
    partial, arrived, halves, peaks, gain, chosen,
    load_sem, field_send, field_recv, green_send, green_recv,
    sum_send, sum_recv, half_send, half_recv, peak_send, peak_recv,
    near, line, everyone,
):
    group = lax.axis_index("group")
    worker = lax.axis_index("worker")
    row, core = group // 2, group % 2

    x, z = worker // LINE, worker % LINE

    def tell(semaphore, dx, dz):
        to = (x + dx) % (WORKERS // LINE) * LINE + (z + dz) % LINE
        pl.semaphore_signal(semaphore, inc=1, device_id={"worker": to}, device_id_type=MESH)

    barrier = pltpu.get_barrier_semaphore()
    for i in range(1, GROUPS):
        pl.semaphore_signal(
            barrier, inc=1, device_id={"group": (group + i) % GROUPS}, device_id_type=MESH
        )
    loads = [
        pltpu.make_async_copy(source, target, load_sem.at[i])
        for i, (source, target) in enumerate(
            [
                (slip_hbm, slip_ref),
                (time_hbm, time_ref),
                (green_hbm, green_ref),
                (periods_hbm, periods_ref),
                (owner_hbm, owner_ref),
            ]
        )
    ]
    for load in loads:
        load.start()
    for dx, dz in ((0, 1), (0, -1), (1, 0), (-1, 0)):
        tell(barrier, dx, dz)

    for load in loads[:3]:
        load.wait()
    with jax.named_scope("stage"):
        for y in range(GROUPS // 2):
            lanes = slice(64 * y, 64 * y + 64)
            field_stage[y] = jnp.concatenate([slip_ref[:, lanes], time_ref[:, lanes]], axis=1)
        for c in range(2):
            for part in range(4):
                start = part * NF + c * HALF
                green_stage[c, :, part * HALF : (part + 1) * HALF] = green_ref[
                    :, start : start + HALF
                ].astype(f32)

    with jax.named_scope("barrier"):
        pl.semaphore_wait(barrier, GROUPS - 1 + 4)

    others, most = pl.ds(0, ROWS * (GROUPS - 1)), pl.ds(0, WORKERS - 1)
    mine = pl.ds(pl.multiple_of(ROWS * group, ROWS), ROWS)
    with jax.named_scope("send_fields"):
        for i in range(1, GROUPS):
            to = (group + i) % GROUPS
            copy = pltpu.make_async_remote_copy(
                src_ref=field_stage.at[to // 2],
                dst_ref=field_all.at[mine],
                send_sem=field_send,
                recv_sem=field_recv,
                device_id={"group": to},
                device_id_type=MESH,
            )
            copy.start()
        for dx, dz in ((0, 1), (0, -1), (1, 0), (-1, 0)):
            tell(near, dx, dz)
        for i in range(1, GROUPS):
            to = (group + i) % GROUPS
            copy = pltpu.make_async_remote_copy(
                src_ref=green_stage.at[to % 2],
                dst_ref=green_all.at[mine],
                send_sem=green_send,
                recv_sem=green_recv,
                device_id={"group": to},
                device_id_type=MESH,
            )
            copy.start()
    field_all[mine, :] = field_stage[row]
    green_all[mine, :] = green_stage[core]

    for load in loads[3:]:
        load.wait()
    with jax.named_scope("gain"):
        natural = (2.0 * math.pi) / periods_ref[...]
        column = jnp.concatenate(
            [
                jnp.transpose(jnp.broadcast_to(natural[:, :128], (128, 128))),
                jnp.transpose(jnp.broadcast_to(natural[:, 128:], (128, 128))),
            ],
            axis=0,
        )
        for h in range(2):
            index = lax.broadcasted_iota(jnp.int32, (NP, 128), 1) + 128 * h
            angular = (2.0 * math.pi) * index.astype(f32) / (NT * TIME_STEP)
            denom_real = column * column - angular * angular
            denom_imag = (2.0 * DAMPING) * column * angular
            scale = column * column / (denom_real * denom_real + denom_imag * denom_imag)
            gain[0, :, 128 * h : 128 * h + 128] = -scale * denom_real
            gain[1, :, 128 * h : 128 * h + 128] = scale * denom_imag

    with jax.named_scope("basis"):
        freq = lax.broadcasted_iota(jnp.int32, (16, NF), 1)
        time = lax.broadcasted_iota(jnp.int32, (16, NF), 0)
        fold = jnp.where(freq == 0, 1.0, 2.0)
        cos0, sin0 = cos_sin_turns((freq * time).astype(f32) * (1.0 / NT))
        cos16, sin16 = cos_sin_turns(freq.astype(f32) * (16.0 / NT))

        def advance(b, carry):
            cos, sin = carry
            rows = pl.ds(pl.multiple_of(16 * b, 16), 16)
            basis[0, rows, :] = cos.astype(bf16)
            basis[1, rows, :] = sin.astype(bf16)
            return cos * cos16 + sin * sin16, sin * cos16 - cos * sin16

        lax.fori_loop(0, TIMES // 16, advance, (fold * cos0, -fold * sin0), unroll=3)

    with jax.named_scope("owners"):
        count = jnp.int32(0)
        for i in range(WORKERS):
            hit = (owner_ref[WORKERS * group + i] == worker).astype(jnp.int32)
            for j in range(MOST):
                value = (hit * (count == j).astype(jnp.int32)).astype(f32)
                chosen[j, i] = jnp.full((4, 128), value, f32)
            count = count + hit

    with jax.named_scope("along_z"):
        pl.semaphore_wait(near, 4)
        for dz in (2, -2):
            tell(line, 0, dz)

    with jax.named_scope("wait_fields"):
        pltpu.make_async_copy(field_all.at[others], field_all.at[others], field_recv).wait()

    with jax.named_scope("phasors"):
        for s in range(0, GATHERED, 32):
            field = field_all[s : s + 32, :]
            swapped = pltpu.roll(field, 64, 1)
            lane = lax.broadcasted_iota(jnp.int32, (32, 128), 1)
            low = lane < 64
            slip = jnp.where(low, field, swapped)
            turn = jnp.where(low, swapped, field) * (1.0 / (NT * TIME_STEP))
            first = (core * HALF + jnp.where(low, 0, STEPS)).astype(f32)
            cos0, sin0 = cos_sin_turns(turn * first)
            cos1, sin1 = cos_sin_turns(turn)

            def step(k, carry, s=s, cos1=cos1, sin1=sin1):
                cos, sin = carry
                phasors[k, s : s + 32, :] = cos.astype(bf16)
                phasors[k, GATHERED + s : GATHERED + s + 32, :] = sin.astype(bf16)
                return cos * cos1 - sin * sin1, sin * cos1 + cos * sin1

            lax.fori_loop(0, STEPS, step, (slip * cos0, slip * sin0), unroll=8)

    with jax.named_scope("along_x"):
        pl.semaphore_wait(line, 2)
        for dx in (1, 2, 3):
            tell(everyone, dx, 0)

    with jax.named_scope("wait_green"):
        pltpu.make_async_copy(green_all.at[others], green_all.at[others], green_recv).wait()

    with jax.named_scope("green"):
        for c in range(2):
            for part in range(2):
                at = (2 * c + part) * HALF
                turned = jnp.transpose(green_all[:, at : at + HALF])
                for h in range(2):
                    value = turned[STEPS * h : STEPS * h + STEPS, :]
                    real = pl.ds(4 * h + 2 * c, STEPS, stride=8)
                    imag = pl.ds(4 * h + 2 * c + 1, STEPS, stride=8)
                    if part == 0:
                        lhs[0, real, :] = value
                        lhs[1, imag, :] = -value
                    else:
                        lhs[1, real, :] = value
                        lhs[0, imag, :] = value

    with jax.named_scope("spectra"):

        def product(k, _):
            rows = pl.ds(pl.multiple_of(16 * k, 16), 16)
            both = jnp.dot(
                jnp.concatenate([lhs[0, rows, :], lhs[1, rows, :]], axis=1).astype(bf16),
                jnp.concatenate([phasors[2 * k], phasors[2 * k + 1]], axis=1),
                preferred_element_type=f32,
            )
            spectra[rows, :] = jnp.concatenate([both[:8, :128], both[8:, 128:]], axis=0)
            return 0

        lax.fori_loop(0, STEPS // 2, product, 0, unroll=4)

    with jax.named_scope("turn"):
        low = lax.broadcasted_iota(jnp.int32, (64, 128), 1) < 64
        for r in range(4):
            both = jnp.concatenate(
                [spectra[pl.ds(r, STEPS, stride=8), :], spectra[pl.ds(4 + r, STEPS, stride=8), :]],
                axis=0,
            )
            turned = jnp.transpose(both)
            value = jnp.where(low, turned[:64], turned[64:])
            for c in range(2):
                partial[pl.ds(4 * c + r, WORKERS, stride=8), :] = value[
                    WORKERS * c : WORKERS * c + WORKERS
                ]

    with jax.named_scope("all_here"):
        pl.semaphore_wait(everyone, 3)

    with jax.named_scope("send_sums"):
        for dx, dz in STEPS_TO:
            to = (x + dx) % (WORKERS // LINE) * LINE + (z + dz) % LINE
            copy = pltpu.make_async_remote_copy(
                src_ref=partial.at[pl.ds(pl.multiple_of(8 * to, 8), 8)],
                dst_ref=arrived.at[worker],
                send_sem=sum_send,
                recv_sem=sum_recv,
                device_id={"worker": to},
                device_id_type=MESH,
            )
            copy.start()
        arrived[worker] = partial[pl.ds(pl.multiple_of(8 * worker, 8), 8), :]
    with jax.named_scope("wait_sums"):
        pltpu.make_async_copy(arrived.at[most], arrived.at[most], sum_recv).wait()

    with jax.named_scope("half"):
        total = arrived[0]
        for i in range(1, WORKERS):
            total = total + arrived[i]
        halves[core] = total
        copy = pltpu.make_async_remote_copy(
            src_ref=halves.at[core],
            dst_ref=halves.at[core],
            send_sem=half_send,
            recv_sem=half_recv,
            device_id={"group": row * 2 + (1 - core)},
            device_id_type=MESH,
        )
        copy.start()
        copy.wait_recv()

    with jax.named_scope("weigh"):
        real, imag = [], []
        for c in range(2):
            for h in range(2):
                spec_real = halves[h, pl.ds(4 * core + 2 * c, 1), :]
                spec_imag = halves[h, pl.ds(4 * core + 2 * c + 1, 1), :]
                gain_real = gain[0, :, 128 * h : 128 * h + 128]
                gain_imag = gain[1, :, 128 * h : 128 * h + 128]
                real.append((spec_real * gain_real - spec_imag * gain_imag).astype(bf16))
                imag.append((spec_real * gain_imag + spec_imag * gain_real).astype(bf16))
        weighted = [
            jnp.concatenate(
                [
                    jnp.concatenate([x[0], x[1]], axis=1),
                    jnp.concatenate([x[2], x[3]], axis=1),
                ],
                axis=0,
            )
            for x in (real, imag)
        ]

    with jax.named_scope("response"):
        contract = (((1,), (1,)), ((), ()))
        best = jnp.zeros((8, 2 * NP), f32)
        for start, size in [(256 * b, 256) for b in range(NT // 512)] + [(NT // 2, 16)]:
            even = lax.dot_general(
                basis[0, start : start + size, :], weighted[0], contract, preferred_element_type=f32
            )
            odd = lax.dot_general(
                basis[1, start : start + size, :], weighted[1], contract, preferred_element_type=f32
            )
            value = jnp.abs(even) + jnp.abs(odd)
            for t in range(0, size, 8):
                best = jnp.maximum(best, value[t : t + 8])
        top = jnp.max(best, axis=0, keepdims=True) * (1.0 / math.sqrt(NF))
        for r in range(4):
            peaks[worker, r : r + 1, :] = top[:, 128 * r : 128 * r + 128]

    with jax.named_scope("send_peaks"):
        for dx, dz in STEPS_TO:
            to = (x + dx) % (WORKERS // LINE) * LINE + (z + dz) % LINE
            copy = pltpu.make_async_remote_copy(
                src_ref=peaks.at[worker],
                dst_ref=peaks.at[worker],
                send_sem=peak_send,
                recv_sem=peak_recv,
                device_id={"worker": to},
                device_id_type=MESH,
            )
            copy.start()
    with jax.named_scope("wait_peaks"):
        pltpu.make_async_copy(peaks.at[most], peaks.at[most], peak_recv).wait()

    with jax.named_scope("place"):
        for j in range(MOST):
            total = chosen[j, 0] * peaks[0]
            for i in range(1, WORKERS):
                total = total + chosen[j, i] * peaks[i]
            for r in range(4):
                out_ref[j : j + 1, 128 * r : 128 * r + 128] = total[r : r + 1, :]

    with jax.named_scope("wait_sent"):
        pltpu.make_async_copy(field_all.at[others], field_all.at[others], field_send).wait()
        pltpu.make_async_copy(green_all.at[others], green_all.at[others], green_send).wait()
        pltpu.make_async_copy(arrived.at[most], arrived.at[most], sum_send).wait()
        pltpu.make_async_copy(halves.at[core], halves.at[core], half_send).wait()
        pltpu.make_async_copy(peaks.at[most], peaks.at[most], peak_send).wait()


def local(green_tensor, slip_field, rupture_time, periods, owner_map):
    vmem = pl.BlockSpec(memory_space=pltpu.VMEM)
    dma = pltpu.SemaphoreType.DMA
    return pl.pallas_call(
        kernel,
        out_shape=jax.ShapeDtypeStruct((MOST, 2 * NP), f32),
        in_specs=[pl.BlockSpec(memory_space=pltpu.HBM)] * 5,
        out_specs=vmem,
        scratch_shapes=[
            pltpu.VMEM((ROWS, 4 * NF), bf16),
            pltpu.VMEM((ROWS, NP), f32),
            pltpu.VMEM((ROWS, NP), f32),
            pltpu.VMEM((1, NP), f32),
            pltpu.SMEM((GROUPS * WORKERS,), jnp.int32),
            pltpu.VMEM((2, TIMES, NF), bf16),
            pltpu.VMEM((2, ROWS, 4 * HALF), f32),
            pltpu.VMEM((GROUPS // 2, ROWS, 128), f32),
            pltpu.VMEM((GATHERED, 4 * HALF), f32),
            pltpu.VMEM((GATHERED, 128), f32),
            pltpu.VMEM((STEPS, 2 * GATHERED, 128), bf16),
            pltpu.VMEM((2, 8 * STEPS, GATHERED), f32),
            pltpu.VMEM((8 * STEPS, 128), f32),
            pltpu.VMEM((8 * WORKERS, 128), f32),
            pltpu.VMEM((WORKERS, 8, 128), f32),
            pltpu.VMEM((2, 8, 128), f32),
            pltpu.VMEM((WORKERS, 4, 128), f32),
            pltpu.VMEM((2, NP, NF), f32),
            pltpu.VMEM((MOST, WORKERS, 4, 128), f32),
        ]
        + [dma((5,))]
        + [dma] * 10
        + [pltpu.SemaphoreType.REGULAR] * 3,
        compiler_params=pltpu.CompilerParams(
            collective_id=0, has_side_effects=True, vmem_limit_bytes=32 * 1024 * 1024
        ),
        name="seismogram",
    )(
        *(
            pltpu.with_memory_space_constraint(x, pltpu.HBM)
            for x in (
                green_tensor,
                slip_field,
                rupture_time,
                periods.reshape(1, NP),
                owner_map.reshape(-1),
            )
        )
    )


def solution(mesh):
    placed = (
        P(("group", "worker"), None),
        P(("group", "worker"), None),
        P(("group", "worker"), None),
        P(),
        P(),
    )
    return jax.shard_map(
        local, mesh=mesh, in_specs=placed, out_specs=P(("group", "worker"), None), check_vma=False
    )
```

```python
import functools
import math

import jax
import jax.numpy as jnp
from jax import lax
from jax.experimental import pallas as pl
from jax.experimental.pallas import tpu as pltpu
from jax.sharding import PartitionSpec as P

NT = 4096
NF = 256
NP = 256
MOST = 3
TIME_STEP = 0.05
DAMPING = 0.05

GROUPS = 8
WORKERS = 32
LINE = 8
ROWS = 16
ORDER = [
    (j, x * LINE + z) for zs in ((0, 1, 2, 3, 7, 6, 5, 4),) for j in range(MOST) for z in zs for x in (0, 1, 3, 2)
]

PARTNERS = 16
GATHERED = ROWS * PARTNERS
QUARTER = 64
STEPS = 32
TIMES = NT // 2 + 16
BLOCKS = [(0, 512), (512, 512), (1024, 512), (1536, 528)]

f32 = jnp.float32
bf16 = jnp.bfloat16
MESH = pl.DeviceIdType.MESH


def cos_sin_turns(turns):
    near = turns - jnp.round(turns)
    angle = near * (2.0 * math.pi)
    square = angle * angle
    cos = f32(0.0)
    for n in range(8, -1, -1):
        cos = cos * square + f32((-1) ** n / math.factorial(2 * n))
    sin = f32(0.0)
    for n in range(8, -1, -1):
        sin = sin * square + f32((-1) ** n / math.factorial(2 * n + 1))
    return cos, sin * angle


def kernel(
    green_hbm, slip_hbm, time_hbm, periods_hbm, owner_hbm, out_ref,
    green_ref, slip_ref, time_ref, periods_ref, owner_ref, basis, green_stage, field_stage, green_all, field_all, phasors, lhs, spectra,
    partial, arrived, gain, chosen,
    load_sem, field_send, field_recv, green_send, green_recv,
    sum_send, sum_recv,
    near, line, everyone,
):
    group = lax.axis_index("group")
    worker = lax.axis_index("worker")
    row, core = group // 2, group % 2

    x, z = worker // LINE, worker % LINE

    def tell(semaphore, dx, dz):
        to = (x + dx) % (WORKERS // LINE) * LINE + (z + dz) % LINE
        pl.semaphore_signal(semaphore, inc=1, device_id={"worker": to}, device_id_type=MESH)

    place = z % 2
    me = 2 * group + place

    def partner(i):
        return {"group": i // 2, "worker": worker - place + i % 2}

    barrier = pltpu.get_barrier_semaphore()
    for i in range(1, PARTNERS):
        pl.semaphore_signal(
            barrier, inc=1, device_id=partner((me + i) % PARTNERS), device_id_type=MESH
        )
    loads = [
        pltpu.make_async_copy(source, target, load_sem.at[i])
        for i, (source, target) in enumerate(
            [
                (slip_hbm, slip_ref),
                (time_hbm, time_ref),
                (green_hbm, green_ref),
                (periods_hbm, periods_ref),
                (owner_hbm, owner_ref),
            ]
        )
    ]
    for load in loads:
        load.start()
    for dx, dz in ((0, 1), (0, -1), (1, 0), (-1, 0)):
        tell(barrier, dx, dz)

    for load in loads[:3]:
        load.wait()
    with jax.named_scope("stage"):
        for y in range(GROUPS // 2):
            lanes = slice(64 * y, 64 * y + 64)
            field_stage[y] = jnp.concatenate([slip_ref[:, lanes], time_ref[:, lanes]], axis=1)
        for part in range(4):
            for quarter in range(4):
                start = part * NF + quarter * QUARTER
                green_stage[quarter, :, part * QUARTER : (part + 1) * QUARTER] = green_ref[
                    :, start : start + QUARTER
                ].astype(f32)

    with jax.named_scope("barrier"):
        pl.semaphore_wait(barrier, PARTNERS - 1 + 4)

    others = pl.ds(0, ROWS * (PARTNERS - 1))
    mine = pl.ds(pl.multiple_of(ROWS * me, ROWS), ROWS)
    with jax.named_scope("send_fields"):
        for to in range(PARTNERS):
            copy = pltpu.make_async_remote_copy(
                src_ref=field_stage.at[to // 4],
                dst_ref=field_all.at[mine],
                send_sem=field_send,
                recv_sem=field_recv,
                device_id=partner(to),
                device_id_type=MESH,
            )
            pl.when(me != to)(copy.start)
        for dx, dz in ((0, 1), (0, -1), (1, 0), (-1, 0)):
            tell(near, dx, dz)
        for to in range(PARTNERS):
            copy = pltpu.make_async_remote_copy(
                src_ref=green_stage.at[to % 4],
                dst_ref=green_all.at[mine],
                send_sem=green_send,
                recv_sem=green_recv,
                device_id=partner(to),
                device_id_type=MESH,
            )
            pl.when(me != to)(copy.start)
    field_all[mine, :] = field_stage[row]
    green_all[mine, :] = green_stage[2 * core + place]

    for load in loads[3:]:
        load.wait()
    with jax.named_scope("gain"):
        natural = (2.0 * math.pi) / periods_ref[...]
        column = jnp.concatenate(
            [
                jnp.transpose(jnp.broadcast_to(natural[:, :128], (128, 128))),
                jnp.transpose(jnp.broadcast_to(natural[:, 128:], (128, 128))),
            ],
            axis=0,
        )
        for h in range(2):
            index = lax.broadcasted_iota(jnp.int32, (NP, 128), 1) + 128 * h
            angular = (2.0 * math.pi) * index.astype(f32) / (NT * TIME_STEP)
            denom_real = column * column - angular * angular
            denom_imag = (2.0 * DAMPING) * column * angular
            scale = column * column / (denom_real * denom_real + denom_imag * denom_imag)
            gain[0, :, 128 * h : 128 * h + 128] = -scale * denom_real
            gain[1, :, 128 * h : 128 * h + 128] = scale * denom_imag

    with jax.named_scope("basis"):
        freq = lax.broadcasted_iota(jnp.int32, (16, NF), 1)
        time = lax.broadcasted_iota(jnp.int32, (16, NF), 0)
        fold = jnp.where(freq == 0, 1.0, 2.0)
        cos0, sin0 = cos_sin_turns((freq * time).astype(f32) * (1.0 / NT))
        cos16, sin16 = cos_sin_turns(freq.astype(f32) * (16.0 / NT))

        def advance(b, carry):
            cos, sin = carry
            rows = pl.ds(pl.multiple_of(16 * b, 16), 16)
            basis[0, rows, :] = cos.astype(bf16)
            basis[1, rows, :] = sin.astype(bf16)
            return cos * cos16 + sin * sin16, sin * cos16 - cos * sin16

        lax.fori_loop(0, TIMES // 16, advance, (fold * cos0, -fold * sin0), unroll=3)

    with jax.named_scope("owners"):
        pair = owner_ref[:, 0:64]
        for y in range(1, GROUPS // 2):
            pair = jnp.where(row == y, owner_ref[:, 64 * y : 64 * y + 64], pair)
        pair = jnp.concatenate([pair, pair], axis=1)
        lane = lax.broadcasted_iota(jnp.int32, (128, 128), 1) % 64
        other = lax.broadcasted_iota(jnp.int32, (128, 128), 0)
        named = jnp.broadcast_to(pair, (128, 128))
        same = (jnp.transpose(named) == named) & (other // WORKERS == lane // WORKERS)
        earlier = jnp.where(same & (other < lane), 1.0, 0.0)
        rank = jnp.sum(earlier, axis=0, keepdims=True).astype(jnp.int32)
        for j in range(MOST):
            for c in range(2):
                lane = lax.broadcasted_iota(jnp.int32, (WORKERS, 128), 1) % 64
                owner = lax.broadcasted_iota(jnp.int32, (WORKERS, 128), 0)
                hit = (pair == owner) & (lane // WORKERS == c) & (rank == j)
                start = (2 * j + c) * WORKERS
                chosen[start : start + WORKERS, :] = jnp.where(hit, 1.0, 0.0).astype(bf16)

    with jax.named_scope("along_z"):
        pl.semaphore_wait(near, 4)
        for dz in (2, -2):
            tell(line, 0, dz)

    with jax.named_scope("wait_fields"):
        pltpu.make_async_copy(field_all.at[others], field_all.at[others], field_recv).wait()

    with jax.named_scope("phasors"):
        for s in range(0, GATHERED, 32):
            field = field_all[s : s + 32, :]
            swapped = pltpu.roll(field, 64, 1)
            lane = lax.broadcasted_iota(jnp.int32, (32, 128), 1)
            low = lane < 64
            slip = jnp.where(low, field, swapped)
            turn = jnp.where(low, swapped, field) * (1.0 / (NT * TIME_STEP))
            first = ((2 * core + place) * QUARTER + jnp.where(low, 0, STEPS)).astype(f32)
            cos0, sin0 = cos_sin_turns(turn * first)
            cos1, sin1 = cos_sin_turns(turn)

            def step(k, carry, s=s, cos1=cos1, sin1=sin1):
                cos, sin = carry
                phasors[k, s : s + 32, :] = cos.astype(bf16)
                phasors[k, GATHERED + s : GATHERED + s + 32, :] = sin.astype(bf16)
                return cos * cos1 - sin * sin1, sin * cos1 + cos * sin1

            lax.fori_loop(0, STEPS, step, (slip * cos0, slip * sin0), unroll=8)

    with jax.named_scope("along_x"):
        pl.semaphore_wait(line, 2)
        for dx in (1, 2, 3):
            tell(everyone, dx, 0)

    with jax.named_scope("wait_green"):
        pltpu.make_async_copy(green_all.at[others], green_all.at[others], green_recv).wait()

    with jax.named_scope("green"):
        for c in range(2):
            for half in range(2):
                turned = jnp.transpose(
                    green_all[128 * half : 128 * half + 128, 128 * c : 128 * c + 128]
                )
                for h in range(2):
                    value = [
                        turned[QUARTER * part + STEPS * h : QUARTER * part + STEPS * h + STEPS, :]
                        for part in range(2)
                    ]
                    real = pl.ds(4 * h + 2 * c, STEPS, stride=8)
                    imag = pl.ds(4 * h + 2 * c + 1, STEPS, stride=8)
                    lhs[half, real, :] = value[0]
                    lhs[half, imag, :] = value[1]
                    lhs[2 + half, real, :] = value[1]
                    lhs[2 + half, imag, :] = -value[0]

    with jax.named_scope("spectra"):

        def product(k, _):
            rows = pl.ds(pl.multiple_of(16 * k, 16), 16)
            both = jnp.dot(
                jnp.concatenate([lhs[i, rows, :] for i in range(4)], axis=1).astype(bf16),
                jnp.concatenate([phasors[2 * k], phasors[2 * k + 1]], axis=1),
                preferred_element_type=f32,
            )
            spectra[rows, :] = jnp.concatenate([both[:8, :128], both[8:, 128:]], axis=0)
            return 0

        lax.fori_loop(0, STEPS // 2, product, 0, unroll=4)

    contract = (((1,), (1,)), ((), ()))
    with jax.named_scope("place"):
        low = lax.broadcasted_iota(jnp.int32, (STEPS, 128), 1) < 64
        for c in range(2):
            parts = []
            for r in (2 * c, 2 * c + 1):
                parts.append(jnp.where(low, spectra[pl.ds(r, STEPS, stride=8), :], 0.0))
                parts.append(jnp.where(low, 0.0, spectra[pl.ds(4 + r, STEPS, stride=8), :]))
            rest = jnp.concatenate(parts, axis=0)
            value = jnp.zeros((2 * MOST * WORKERS, 128), f32)
            for _ in range(3):
                piece = rest.astype(bf16)
                rest = rest - piece.astype(f32)
                value = value + lax.dot_general(
                    chosen[...], piece, contract, preferred_element_type=f32
                )
            for block in range(2 * MOST):
                partial[pl.ds(2 * WORKERS * block + c, WORKERS, stride=2), :] = value[
                    WORKERS * block : WORKERS * block + WORKERS
                ]

    with jax.named_scope("all_here"):
        pl.semaphore_wait(everyone, 3)

    def part(j, c, w):
        return pl.ds(pl.multiple_of(2 * (WORKERS * (2 * j + c) + w), 2), 2)

    with jax.named_scope("send_sums"):
        for j, to in ORDER:
            for c in (1, 0):
                copy = pltpu.make_async_remote_copy(
                    src_ref=partial.at[part(j, c, to)],
                    dst_ref=arrived.at[j, part(0, core, worker)],
                    send_sem=sum_send,
                    recv_sem=sum_recv.at[j],
                    device_id={"group": 2 * row + c, "worker": to},
                    device_id_type=MESH,
                )
                pl.when((worker != to) | (core != c))(copy.start)
        for j in range(MOST):
            arrived[j, part(0, core, worker), :] = partial[part(j, core, worker), :]

    most = pl.ds(0, 2 * (2 * WORKERS - 1))
    for j in range(MOST):
        with jax.named_scope("wait_sums"):
            pltpu.make_async_copy(
                arrived.at[j, most], arrived.at[j, most], sum_recv.at[j]
            ).wait()

        with jax.named_scope("weigh"):
            spec = []
            for h in range(2):
                total = arrived[j, 2 * WORKERS * h : 2 * WORKERS * h + 8, :]
                for i in range(8, 2 * WORKERS, 8):
                    total = total + arrived[j, 2 * WORKERS * h + i : 2 * WORKERS * h + i + 8, :]
                spec.append(total[:4] + total[4:])
            real, imag = [], []
            for c in range(2):
                for h in range(2):
                    near_part, far_part = spec[h][c : c + 1], spec[h][2 + c : 3 + c]
                    spec_real = jnp.concatenate([near_part[:, :64], far_part[:, :64]], axis=1)
                    spec_imag = jnp.concatenate([near_part[:, 64:], far_part[:, 64:]], axis=1)
                    gain_real = gain[0, :, 128 * h : 128 * h + 128]
                    gain_imag = gain[1, :, 128 * h : 128 * h + 128]
                    real.append((spec_real * gain_real - spec_imag * gain_imag).astype(bf16))
                    imag.append((spec_real * gain_imag + spec_imag * gain_real).astype(bf16))
            weighted = [
                [jnp.concatenate(v[2 * c : 2 * c + 2], axis=1) for v in (real, imag)]
                for c in range(2)
            ]

        with jax.named_scope("response"):
            for c in range(2):
                best = jnp.zeros((8, NP), f32)
                for start, size in BLOCKS:
                    even, odd = [
                        lax.dot_general(
                            basis[i, start : start + size, :],
                            weighted[c][i],
                            contract,
                            preferred_element_type=f32,
                        )
                        for i in range(2)
                    ]
                    value = jnp.abs(even) + jnp.abs(odd)
                    for t in range(0, size, 8):
                        best = jnp.maximum(best, value[t : t + 8])
                top = jnp.max(best, axis=0, keepdims=True) * (1.0 / math.sqrt(NF))
                out_ref[j : j + 1, NP * c : NP * c + NP] = top

    with jax.named_scope("wait_sent"):
        pltpu.make_async_copy(field_all.at[others], field_all.at[others], field_send).wait()
        pltpu.make_async_copy(green_all.at[others], green_all.at[others], green_send).wait()
        for j in range(MOST):
            pltpu.make_async_copy(arrived.at[j, most], arrived.at[j, most], sum_send).wait()


def local(green_tensor, slip_field, rupture_time, periods, owner_map):
    vmem = pl.BlockSpec(memory_space=pltpu.VMEM)
    dma = pltpu.SemaphoreType.DMA
    return pl.pallas_call(
        kernel,
        out_shape=jax.ShapeDtypeStruct((MOST, 2 * NP), f32),
        in_specs=[pl.BlockSpec(memory_space=pltpu.HBM)] * 5,
        out_specs=vmem,
        scratch_shapes=[
            pltpu.VMEM((ROWS, 4 * NF), bf16),
            pltpu.VMEM((ROWS, NP), f32),
            pltpu.VMEM((ROWS, NP), f32),
            pltpu.VMEM((1, NP), f32),
            pltpu.VMEM((1, GROUPS * WORKERS), jnp.int32),
            pltpu.VMEM((2, TIMES, NF), bf16),
            pltpu.VMEM((4, ROWS, 4 * QUARTER), f32),
            pltpu.VMEM((GROUPS // 2, ROWS, 128), f32),
            pltpu.VMEM((GATHERED, 4 * QUARTER), f32),
            pltpu.VMEM((GATHERED, 128), f32),
            pltpu.VMEM((STEPS, 2 * GATHERED, 128), bf16),
            pltpu.VMEM((4, 8 * STEPS, 128), f32),
            pltpu.VMEM((8 * STEPS, 128), f32),
            pltpu.VMEM((2 * 2 * MOST * WORKERS, 128), f32),
            pltpu.VMEM((MOST, 2 * 2 * WORKERS, 128), f32),
            pltpu.VMEM((2, NP, NF), f32),
            pltpu.VMEM((2 * MOST * WORKERS, 128), bf16),
        ]
        + [dma((5,))]
        + [dma] * 5 + [dma((MOST,))]
        + [pltpu.SemaphoreType.REGULAR] * 3,
        compiler_params=pltpu.CompilerParams(
            collective_id=0, has_side_effects=True, vmem_limit_bytes=32 * 1024 * 1024
        ),
        name="seismogram",
    )(
        *(
            pltpu.with_memory_space_constraint(x, pltpu.HBM)
            for x in (
                green_tensor,
                slip_field,
                rupture_time,
                periods.reshape(1, NP),
                owner_map.reshape(1, -1),
            )
        )
    )


def solution(mesh):
    placed = (
        P(("group", "worker"), None),
        P(("group", "worker"), None),
        P(("group", "worker"), None),
        P(),
        P(),
    )
    return jax.shard_map(
        local, mesh=mesh, in_specs=placed, out_specs=P(("group", "worker"), None), check_vma=False
    )
```

```python
import functools
import math

import jax
import jax.numpy as jnp
from jax import lax
from jax.experimental import pallas as pl
from jax.experimental.pallas import tpu as pltpu
from jax.sharding import PartitionSpec as P

NT = 4096
NF = 256
NP = 256
MOST = 3
TIME_STEP = 0.05
DAMPING = 0.05

GROUPS = 8
WORKERS = 32
LINE = 8
ROWS = 16
EXTRA = (MOST - 1, 0, 1)
ORDER = [
    (j, x * LINE + z, c)
    for j in range(MOST)
    for z in (0, 1, 2, 3, 7, 6, 5, 4)
    for x in (0, 1, 3, 2)
    for c in (1, 0)
]
ORDER.remove(EXTRA)
ORDER.insert(1, EXTRA)
PARTNERS = 16
GATHERED = ROWS * PARTNERS
BAND = 64
UNROLL = 8
QUARTER = 64
STEPS = 32
TIMES = NT // 2 + 16
BLOCKS = [(0, 512), (512, 512), (1024, 512), (1536, 528)]

f32 = jnp.float32
bf16 = jnp.bfloat16
MESH = pl.DeviceIdType.MESH


def cos_sin_turns(turns):
    near = turns - jnp.round(turns)
    angle = near * (2.0 * math.pi)
    square = angle * angle
    cos = f32(0.0)
    for n in range(8, -1, -1):
        cos = cos * square + f32((-1) ** n / math.factorial(2 * n))
    sin = f32(0.0)
    for n in range(8, -1, -1):
        sin = sin * square + f32((-1) ** n / math.factorial(2 * n + 1))
    return cos, sin * angle


def kernel(
    green_hbm, slip_hbm, time_hbm, periods_hbm, owner_hbm, out_ref,
    green_ref, slip_ref, time_ref, periods_ref, owner_ref, basis, green_stage, field_stage, green_all, field_all, phasors, lhs, spectra,
    partial, arrived, gain, chosen, given,
    load_sem, field_send, field_recv, green_send, green_recv,
    sum_send, sum_recv, give_send, give_recv,
    near, line, everyone,
):
    group = lax.axis_index("group")
    worker = lax.axis_index("worker")
    row, core = group // 2, group % 2

    x, z = worker // LINE, worker % LINE

    def tell(semaphore, dx, dz):
        to = (x + dx) % (WORKERS // LINE) * LINE + (z + dz) % LINE
        pl.semaphore_signal(semaphore, inc=1, device_id={"worker": to}, device_id_type=MESH)

    place = z % 2
    helped = (row == 0) & (worker == 0) & (core == 1)
    helper = (row == 0) & (worker == 0) & (core == 0)
    me = 2 * group + place

    def partner(i):
        return {"group": i // 2, "worker": worker - place + i % 2}

    barrier = pltpu.get_barrier_semaphore()
    for i in range(1, PARTNERS):
        pl.semaphore_signal(
            barrier, inc=1, device_id=partner((me + i) % PARTNERS), device_id_type=MESH
        )
    loads = [
        pltpu.make_async_copy(source, target, load_sem.at[i])
        for i, (source, target) in enumerate(
            [
                (slip_hbm, slip_ref),
                (time_hbm, time_ref),
                (green_hbm, green_ref),
                (periods_hbm, periods_ref),
                (owner_hbm, owner_ref),
            ]
        )
    ]
    for load in loads:
        load.start()
    for dx, dz in ((0, 1), (0, -1), (1, 0), (-1, 0)):
        tell(barrier, dx, dz)

    for load in loads[:3]:
        load.wait()
    with jax.named_scope("stage"):
        for y in range(GROUPS // 2):
            lanes = slice(64 * y, 64 * y + 64)
            field_stage[y] = jnp.concatenate([slip_ref[:, lanes], time_ref[:, lanes]], axis=1)
        for part in range(4):
            for quarter in range(4):
                start = part * NF + quarter * QUARTER
                green_stage[quarter, :, part * QUARTER : (part + 1) * QUARTER] = green_ref[
                    :, start : start + QUARTER
                ].astype(f32)

    with jax.named_scope("barrier"):
        pl.semaphore_wait(barrier, PARTNERS - 1 + 4)

    own = pl.ds(pl.multiple_of(ROWS * (2 * core + place), ROWS), ROWS)

    def spot(to):
        away = (row - to // 4 + 4) % 4
        return away + away // 2 * (5 - 2 * away)

    with jax.named_scope("send_fields"):
        for to in range(PARTNERS):
            rows = pl.ds(pl.multiple_of(BAND * spot(to) + ROWS * (2 * core + place), ROWS), ROWS)
            copy = pltpu.make_async_remote_copy(
                src_ref=field_stage.at[to // 4],
                dst_ref=field_all.at[rows],
                send_sem=field_send,
                recv_sem=field_recv.at[spot(to)],
                device_id=partner(to),
                device_id_type=MESH,
            )
            pl.when(me != to)(copy.start)
        for dx, dz in ((0, 1), (0, -1), (1, 0), (-1, 0)):
            tell(near, dx, dz)
        for to in range(PARTNERS):
            rows = pl.ds(pl.multiple_of(BAND * spot(to) + ROWS * (2 * core + place), ROWS), ROWS)
            copy = pltpu.make_async_remote_copy(
                src_ref=green_stage.at[to % 4],
                dst_ref=green_all.at[rows],
                send_sem=green_send,
                recv_sem=green_recv.at[spot(to) // 2],
                device_id=partner(to),
                device_id_type=MESH,
            )
            pl.when(me != to)(copy.start)
    field_all[own, :] = field_stage[row]
    green_all[own, :] = green_stage[2 * core + place]

    for load in loads[3:]:
        load.wait()
    with jax.named_scope("gain"):
        natural = (2.0 * math.pi) / periods_ref[...]
        column = jnp.concatenate(
            [
                jnp.transpose(jnp.broadcast_to(natural[:, :128], (128, 128))),
                jnp.transpose(jnp.broadcast_to(natural[:, 128:], (128, 128))),
            ],
            axis=0,
        )
        for h in range(2):
            index = lax.broadcasted_iota(jnp.int32, (NP, 128), 1) + 128 * h
            angular = (2.0 * math.pi) * index.astype(f32) / (NT * TIME_STEP)
            denom_real = column * column - angular * angular
            denom_imag = (2.0 * DAMPING) * column * angular
            scale = column * column / (denom_real * denom_real + denom_imag * denom_imag)
            gain[0, :, 128 * h : 128 * h + 128] = -scale * denom_real
            gain[1, :, 128 * h : 128 * h + 128] = scale * denom_imag

    with jax.named_scope("basis"):
        freq = lax.broadcasted_iota(jnp.int32, (16, NF), 1)
        time = lax.broadcasted_iota(jnp.int32, (16, NF), 0)
        fold = jnp.where(freq == 0, 1.0, 2.0)
        cos0, sin0 = cos_sin_turns((freq * time).astype(f32) * (1.0 / NT))
        cos16, sin16 = cos_sin_turns(freq.astype(f32) * (16.0 / NT))

        def advance(b, carry):
            cos, sin = carry
            rows = pl.ds(pl.multiple_of(16 * b, 16), 16)
            basis[0, rows, :] = cos.astype(bf16)
            basis[1, rows, :] = sin.astype(bf16)
            return cos * cos16 + sin * sin16, sin * cos16 - cos * sin16

        lax.fori_loop(0, TIMES // 16, advance, (fold * cos0, -fold * sin0), unroll=3)

    with jax.named_scope("owners"):
        pair = owner_ref[:, 0:64]
        for y in range(1, GROUPS // 2):
            pair = jnp.where(row == y, owner_ref[:, 64 * y : 64 * y + 64], pair)
        pair = jnp.concatenate([pair, pair], axis=1)
        lane = lax.broadcasted_iota(jnp.int32, (128, 128), 1) % 64
        other = lax.broadcasted_iota(jnp.int32, (128, 128), 0)
        named = jnp.broadcast_to(pair, (128, 128))
        same = (jnp.transpose(named) == named) & (other // WORKERS == lane // WORKERS)
        earlier = jnp.where(same & (other < lane), 1.0, 0.0)
        rank = jnp.sum(earlier, axis=0, keepdims=True).astype(jnp.int32)
        for j in range(MOST):
            for c in range(2):
                lane = lax.broadcasted_iota(jnp.int32, (WORKERS, 128), 1) % 64
                owner = lax.broadcasted_iota(jnp.int32, (WORKERS, 128), 0)
                hit = (pair == owner) & (lane // WORKERS == c) & (rank == j)
                start = (2 * j + c) * WORKERS
                chosen[start : start + WORKERS, :] = jnp.where(hit, 1.0, 0.0).astype(bf16)

    with jax.named_scope("along_z"):
        pl.semaphore_wait(near, 4)
        for dz in (2, -2):
            tell(line, 0, dz)

    for band in range(4):
        with jax.named_scope("wait_fields"):
            arriving = pl.ds(BAND * band, BAND - ROWS if band == 0 else BAND)
            pltpu.make_async_copy(
                field_all.at[arriving], field_all.at[arriving], field_recv.at[band]
            ).wait()

        with jax.named_scope("phasors"):
            for s in range(BAND * band, BAND * band + BAND, 32):
                field = field_all[s : s + 32, :]
                swapped = pltpu.roll(field, 64, 1)
                lane = lax.broadcasted_iota(jnp.int32, (32, 128), 1)
                low = lane < 64
                slip = jnp.where(low, field, swapped)
                turn = jnp.where(low, swapped, field) * (1.0 / (NT * TIME_STEP))
                first = ((2 * core + place) * QUARTER + jnp.where(low, 0, STEPS)).astype(f32)
                cos0, sin0 = cos_sin_turns(turn * first)
                cos1, sin1 = cos_sin_turns(turn)
                at = s + s // 128 * 128

                def step(k, carry, at=at, cos1=cos1, sin1=sin1):
                    cos, sin = carry
                    phasors[k, at : at + 32, :] = cos.astype(bf16)
                    phasors[k, at + 128 : at + 160, :] = sin.astype(bf16)
                    return cos * cos1 - sin * sin1, sin * cos1 + cos * sin1

                lax.fori_loop(0, STEPS, step, (slip * cos0, slip * sin0), unroll=8)

    with jax.named_scope("along_x"):
        pl.semaphore_wait(line, 2)
        for dx in (1, 2, 3):
            tell(everyone, dx, 0)

    for half in range(2):
        with jax.named_scope("wait_green"):
            arriving = pl.ds(128 * half, 128 - ROWS if half == 0 else 128)
            pltpu.make_async_copy(
                green_all.at[arriving], green_all.at[arriving], green_recv.at[half]
            ).wait()

        with jax.named_scope("green"):
            for c in range(2):
                turned = jnp.transpose(
                    green_all[128 * half : 128 * half + 128, 128 * c : 128 * c + 128]
                )
                for h in range(2):
                    value = [
                        turned[QUARTER * part + STEPS * h : QUARTER * part + STEPS * h + STEPS, :]
                        for part in range(2)
                    ]
                    real = pl.ds(4 * h + 2 * c, STEPS, stride=8)
                    imag = pl.ds(4 * h + 2 * c + 1, STEPS, stride=8)
                    lhs[2 * half, real, :] = value[0]
                    lhs[2 * half, imag, :] = value[1]
                    lhs[2 * half + 1, real, :] = value[1]
                    lhs[2 * half + 1, imag, :] = -value[0]

        with jax.named_scope("spectra"):

            def product(k, _, half=half):
                rows = pl.ds(pl.multiple_of(16 * k, 16), 16)
                depth = slice(256 * half, 256 * half + 256)
                both = jnp.dot(
                    jnp.concatenate([lhs[2 * half + i, rows, :] for i in range(2)], axis=1).astype(
                        bf16
                    ),
                    jnp.concatenate(
                        [phasors[2 * k, depth, :], phasors[2 * k + 1, depth, :]], axis=1
                    ),
                    preferred_element_type=f32,
                )
                value = jnp.concatenate([both[:8, :128], both[8:, 128:]], axis=0)
                spectra[rows, :] = value if half == 0 else spectra[rows, :] + value
                return 0

            lax.fori_loop(0, STEPS // 2, product, 0, unroll=UNROLL)

    contract = (((1,), (1,)), ((), ()))
    with jax.named_scope("place"):
        low = lax.broadcasted_iota(jnp.int32, (STEPS, 128), 1) < 64
        for c in range(2):
            parts = []
            for r in (2 * c, 2 * c + 1):
                parts.append(jnp.where(low, spectra[pl.ds(r, STEPS, stride=8), :], 0.0))
                parts.append(jnp.where(low, 0.0, spectra[pl.ds(4 + r, STEPS, stride=8), :]))
            rest = jnp.concatenate(parts, axis=0)
            value = jnp.zeros((2 * MOST * WORKERS, 128), f32)
            for _ in range(3):
                piece = rest.astype(bf16)
                rest = rest - piece.astype(f32)
                value = value + lax.dot_general(
                    chosen[...], piece, contract, preferred_element_type=f32
                )
            for block in range(2 * MOST):
                partial[pl.ds(2 * WORKERS * block + c, WORKERS, stride=2), :] = value[
                    WORKERS * block : WORKERS * block + WORKERS
                ]

    with jax.named_scope("all_here"):
        pl.semaphore_wait(everyone, 3)

    def part(j, c, w):
        return pl.ds(pl.multiple_of(2 * (WORKERS * (2 * j + c) + w), 2), 2)

    with jax.named_scope("send_sums"):
        for j, to, c in ORDER:
            slot, source = j, partial.at[part(j, c, to)]
            if (j, to, c) == EXTRA:
                aside = jnp.where(row == 0, 1, 0)
                slot, c = j + aside, c - aside
            copy = pltpu.make_async_remote_copy(
                src_ref=source,
                dst_ref=arrived.at[slot, part(0, core, worker)],
                send_sem=sum_send,
                recv_sem=sum_recv.at[slot],
                device_id={"group": 2 * row + c, "worker": to},
                device_id_type=MESH,
            )
            pl.when((worker != to) | (core != c))(copy.start)
        for j in range(MOST):
            arrived[j, part(0, core, worker), :] = partial[part(j, core, worker), :]

        @pl.when(helper)
        def _():
            arrived[MOST, part(0, core, worker), :] = partial[part(MOST - 1, 1, worker), :]

    most = pl.ds(0, 2 * (2 * WORKERS - 1))
    def peaks(j):
        with jax.named_scope("wait_sums"):
            pltpu.make_async_copy(
                arrived.at[j, most], arrived.at[j, most], sum_recv.at[j]
            ).wait()

        with jax.named_scope("weigh"):
            spec = []
            for h in range(2):
                total = arrived[j, 2 * WORKERS * h : 2 * WORKERS * h + 8, :]
                for i in range(8, 2 * WORKERS, 8):
                    total = total + arrived[j, 2 * WORKERS * h + i : 2 * WORKERS * h + i + 8, :]
                spec.append(total[:4] + total[4:])
            real, imag = [], []
            for c in range(2):
                for h in range(2):
                    near_part, far_part = spec[h][c : c + 1], spec[h][2 + c : 3 + c]
                    spec_real = jnp.concatenate([near_part[:, :64], far_part[:, :64]], axis=1)
                    spec_imag = jnp.concatenate([near_part[:, 64:], far_part[:, 64:]], axis=1)
                    gain_real = gain[0, :, 128 * h : 128 * h + 128]
                    gain_imag = gain[1, :, 128 * h : 128 * h + 128]
                    real.append((spec_real * gain_real - spec_imag * gain_imag).astype(bf16))
                    imag.append((spec_real * gain_imag + spec_imag * gain_real).astype(bf16))
            weighted = [
                [jnp.concatenate(v[2 * c : 2 * c + 2], axis=1) for v in (real, imag)]
                for c in range(2)
            ]

        with jax.named_scope("response"):
            tops = []
            for c in range(2):
                best = jnp.zeros((8, NP), f32)
                for start, size in BLOCKS:
                    even, odd = [
                        lax.dot_general(
                            basis[i, start : start + size, :],
                            weighted[c][i],
                            contract,
                            preferred_element_type=f32,
                        )
                        for i in range(2)
                    ]
                    value = jnp.abs(even) + jnp.abs(odd)
                    for t in range(0, size, 8):
                        best = jnp.maximum(best, value[t : t + 8])
                tops.append(jnp.max(best, axis=0, keepdims=True) * (1.0 / math.sqrt(NF)))
        return jnp.concatenate(tops, axis=1)

    give = pltpu.make_async_remote_copy(
        src_ref=given,
        dst_ref=given,
        send_sem=give_send,
        recv_sem=give_recv,
        device_id={"group": 2 * row + 1 - core},
        device_id_type=MESH,
    )

    @pl.when(helper)
    def _():
        given[...] = peaks(MOST)
        give.start()

    for j in range(MOST - 1):
        out_ref[j : j + 1, :] = peaks(j)

    @pl.when(jnp.logical_not(helped))
    def _():
        out_ref[MOST - 1 : MOST, :] = peaks(MOST - 1)

    @pl.when(helped)
    def _():
        give.wait_recv()
        out_ref[MOST - 1 : MOST, :] = given[...]

    with jax.named_scope("wait_sent"):
        others = pl.ds(0, ROWS * (PARTNERS - 1))
        pltpu.make_async_copy(field_all.at[others], field_all.at[others], field_send).wait()
        pltpu.make_async_copy(green_all.at[others], green_all.at[others], green_send).wait()
        for j in range(MOST - 1):
            pltpu.make_async_copy(arrived.at[j, most], arrived.at[j, most], sum_send).wait()
        fewer, one = pl.ds(0, 2 * (2 * WORKERS - 2)), pl.ds(0, 2)
        pltpu.make_async_copy(arrived.at[0, fewer], arrived.at[0, fewer], sum_send).wait()
        last = pltpu.make_async_copy(arrived.at[0, one], arrived.at[0, one], sum_send)
        pl.when(jnp.logical_not(helper))(last.wait)
        pl.when(helped)(last.wait)
        pl.when(helper)(give.wait_send)


def local(green_tensor, slip_field, rupture_time, periods, owner_map):
    vmem = pl.BlockSpec(memory_space=pltpu.VMEM)
    dma = pltpu.SemaphoreType.DMA
    return pl.pallas_call(
        kernel,
        out_shape=jax.ShapeDtypeStruct((MOST, 2 * NP), f32),
        in_specs=[pl.BlockSpec(memory_space=pltpu.HBM)] * 5,
        out_specs=vmem,
        scratch_shapes=[
            pltpu.VMEM((ROWS, 4 * NF), bf16),
            pltpu.VMEM((ROWS, NP), f32),
            pltpu.VMEM((ROWS, NP), f32),
            pltpu.VMEM((1, NP), f32),
            pltpu.VMEM((1, GROUPS * WORKERS), jnp.int32),
            pltpu.VMEM((2, TIMES, NF), bf16),
            pltpu.VMEM((4, ROWS, 4 * QUARTER), f32),
            pltpu.VMEM((GROUPS // 2, ROWS, 128), f32),
            pltpu.VMEM((GATHERED, 4 * QUARTER), f32),
            pltpu.VMEM((GATHERED, 128), f32),
            pltpu.VMEM((STEPS, 2 * GATHERED, 128), bf16),
            pltpu.VMEM((4, 8 * STEPS, 128), f32),
            pltpu.VMEM((8 * STEPS, 128), f32),
            pltpu.VMEM((2 * 2 * MOST * WORKERS, 128), f32),
            pltpu.VMEM((MOST + 1, 2 * 2 * WORKERS, 128), f32),
            pltpu.VMEM((2, NP, NF), f32),
            pltpu.VMEM((2 * MOST * WORKERS, 128), bf16),
            pltpu.VMEM((1, 2 * NP), f32),
        ]
        + [dma((5,)), dma, dma((4,)), dma, dma((2,)), dma, dma((MOST + 1,)), dma, dma]
        + [pltpu.SemaphoreType.REGULAR] * 3,
        compiler_params=pltpu.CompilerParams(
            collective_id=0, has_side_effects=True, vmem_limit_bytes=32 * 1024 * 1024
        ),
        name="seismogram",
    )(
        *(
            pltpu.with_memory_space_constraint(x, pltpu.HBM)
            for x in (
                green_tensor,
                slip_field,
                rupture_time,
                periods.reshape(1, NP),
                owner_map.reshape(1, -1),
            )
        )
    )


def solution(mesh):
    placed = (
        P(("group", "worker"), None),
        P(("group", "worker"), None),
        P(("group", "worker"), None),
        P(),
        P(),
    )
    return jax.shard_map(
        local, mesh=mesh, in_specs=placed, out_specs=P(("group", "worker"), None), check_vma=False
    )
```

```python
import functools
import math

import jax
import jax.numpy as jnp
from jax import lax
from jax.experimental import pallas as pl
from jax.experimental.pallas import tpu as pltpu
from jax.sharding import PartitionSpec as P

NT = 4096
NF = 256
NP = 256
MOST = 3
TIME_STEP = 0.05
DAMPING = 0.05

GROUPS = 8
WORKERS = 32
LINE = 8
ROWS = 16
EXTRA = (MOST - 1, 0, 1)
ORDER = [
    (j, x * LINE + z, c)
    for j in range(MOST)
    for z in (0, 1, 2, 3, 7, 6, 5, 4)
    for x in (0, 1, 3, 2)
    for c in (1, 0)
]
ORDER.remove(EXTRA)
ORDER.insert(1, EXTRA)
SENDS = [(to, 0) for to in (0, 1, 2, 3, 12, 13, 14, 15, 8, 9, 10, 11, 4, 5, 6, 7)] + [
    (to, 1) for to in (0, 1, 2, 3, 12, 13, 14, 15, 8, 9, 10, 11, 4, 5, 6, 7)
]
PARTNERS = 16
GATHERED = ROWS * PARTNERS
BAND = 64
UNROLL = 16
QUARTER = 64
STEPS = 32
TIMES = NT // 2 + 16
BLOCKS = [(0, 512), (512, 512), (1024, 512), (1536, 528)]

f32 = jnp.float32
bf16 = jnp.bfloat16
MESH = pl.DeviceIdType.MESH


def cos_sin_turns(turns):
    near = turns - jnp.round(turns)
    angle = near * (2.0 * math.pi)
    square = angle * angle
    cos = f32(0.0)
    for n in range(8, -1, -1):
        cos = cos * square + f32((-1) ** n / math.factorial(2 * n))
    sin = f32(0.0)
    for n in range(8, -1, -1):
        sin = sin * square + f32((-1) ** n / math.factorial(2 * n + 1))
    return cos, sin * angle


def kernel(
    green_hbm, slip_hbm, time_hbm, periods_hbm, owner_hbm, out_ref,
    green_ref, slip_ref, time_ref, periods_ref, owner_ref, basis, green_stage, field_stage, green_all, field_all, phasors, lhs, spectra,
    partial, arrived, gain, chosen, given,
    load_sem, field_send, field_recv, green_send, green_recv,
    sum_send, sum_recv, give_send, give_recv,
    near, line, everyone,
):
    group = lax.axis_index("group")
    worker = lax.axis_index("worker")
    row, core = group // 2, group % 2

    x, z = worker // LINE, worker % LINE

    def tell(semaphore, dx, dz):
        to = (x + dx) % (WORKERS // LINE) * LINE + (z + dz) % LINE
        pl.semaphore_signal(semaphore, inc=1, device_id={"worker": to}, device_id_type=MESH)

    place = z % 2
    helped = (row == 0) & (worker == 0) & (core == 1)
    helper = (row == 0) & (worker == 0) & (core == 0)
    me = 2 * group + place

    def partner(i):
        return {"group": i // 2, "worker": worker - place + i % 2}

    barrier = pltpu.get_barrier_semaphore()
    for i in range(1, PARTNERS):
        pl.semaphore_signal(
            barrier, inc=1, device_id=partner((me + i) % PARTNERS), device_id_type=MESH
        )
    loads = [
        pltpu.make_async_copy(source, target, load_sem.at[i])
        for i, (source, target) in enumerate(
            [
                (slip_hbm, slip_ref),
                (time_hbm, time_ref),
                (green_hbm, green_ref),
                (periods_hbm, periods_ref),
                (owner_hbm, owner_ref),
            ]
        )
    ]
    for load in loads:
        load.start()
    for dx, dz in ((0, 1), (0, -1), (1, 0), (-1, 0)):
        tell(barrier, dx, dz)

    for load in loads[:3]:
        load.wait()
    with jax.named_scope("stage"):
        for y in range(GROUPS // 2):
            lanes = slice(64 * y, 64 * y + 64)
            field_stage[y] = jnp.concatenate([slip_ref[:, lanes], time_ref[:, lanes]], axis=1)
        for part in range(4):
            for quarter in range(4):
                start = part * NF + quarter * QUARTER
                green_stage[quarter, :, part * QUARTER : (part + 1) * QUARTER] = green_ref[
                    :, start : start + QUARTER
                ].astype(f32)

    with jax.named_scope("barrier"):
        pl.semaphore_wait(barrier, PARTNERS - 1 + 4)

    own = pl.ds(pl.multiple_of(ROWS * (2 * core + place), ROWS), ROWS)

    def spot(to):
        away = (row - to // 4 + 4) % 4
        return away + away // 2 * (5 - 2 * away)

    def send(to, which):
        rows = pl.ds(pl.multiple_of(BAND * spot(to) + ROWS * (2 * core + place), ROWS), ROWS)
        if which == 0:
            source, target = field_stage.at[to // 4], field_all.at[rows]
            sent, received = field_send, field_recv.at[spot(to)]
        else:
            source, target = green_stage.at[to % 4], green_all.at[rows]
            sent, received = green_send, green_recv.at[spot(to) // 2]
        pltpu.make_async_remote_copy(
            src_ref=source,
            dst_ref=target,
            send_sem=sent,
            recv_sem=received,
            device_id=partner(to),
            device_id_type=MESH,
        ).start()

    with jax.named_scope("send_inputs"):
        for to, which in SENDS:
            pl.when(me != to)(functools.partial(send, to, which))
        for dx, dz in ((0, 1), (0, -1), (1, 0), (-1, 0)):
            tell(near, dx, dz)
    field_all[own, :] = field_stage[row]
    green_all[own, :] = green_stage[2 * core + place]

    for load in loads[3:]:
        load.wait()
    with jax.named_scope("gain"):
        natural = (2.0 * math.pi) / periods_ref[...]
        column = jnp.concatenate(
            [
                jnp.transpose(jnp.broadcast_to(natural[:, :128], (128, 128))),
                jnp.transpose(jnp.broadcast_to(natural[:, 128:], (128, 128))),
            ],
            axis=0,
        )
        for h in range(2):
            index = lax.broadcasted_iota(jnp.int32, (NP, 128), 1) + 128 * h
            angular = (2.0 * math.pi) * index.astype(f32) / (NT * TIME_STEP)
            denom_real = column * column - angular * angular
            denom_imag = (2.0 * DAMPING) * column * angular
            scale = column * column / (denom_real * denom_real + denom_imag * denom_imag)
            gain[0, :, 128 * h : 128 * h + 128] = -scale * denom_real
            gain[1, :, 128 * h : 128 * h + 128] = scale * denom_imag

    with jax.named_scope("basis"):
        freq = lax.broadcasted_iota(jnp.int32, (16, NF), 1)
        time = lax.broadcasted_iota(jnp.int32, (16, NF), 0)
        fold = jnp.where(freq == 0, 1.0, 2.0)
        cos0, sin0 = cos_sin_turns((freq * time).astype(f32) * (1.0 / NT))
        cos16, sin16 = cos_sin_turns(freq.astype(f32) * (16.0 / NT))

        def advance(b, carry):
            cos, sin = carry
            rows = pl.ds(pl.multiple_of(16 * b, 16), 16)
            basis[0, rows, :] = cos.astype(bf16)
            basis[1, rows, :] = sin.astype(bf16)
            return cos * cos16 + sin * sin16, sin * cos16 - cos * sin16

        lax.fori_loop(0, TIMES // 16, advance, (fold * cos0, -fold * sin0), unroll=3)

    with jax.named_scope("owners"):
        pair = owner_ref[:, 0:64]
        for y in range(1, GROUPS // 2):
            pair = jnp.where(row == y, owner_ref[:, 64 * y : 64 * y + 64], pair)
        pair = jnp.concatenate([pair, pair], axis=1)
        lane = lax.broadcasted_iota(jnp.int32, (128, 128), 1) % 64
        other = lax.broadcasted_iota(jnp.int32, (128, 128), 0)
        named = jnp.broadcast_to(pair, (128, 128))
        same = (jnp.transpose(named) == named) & (other // WORKERS == lane // WORKERS)
        earlier = jnp.where(same & (other < lane), 1.0, 0.0)
        rank = jnp.sum(earlier, axis=0, keepdims=True).astype(jnp.int32)
        for j in range(MOST):
            for c in range(2):
                lane = lax.broadcasted_iota(jnp.int32, (WORKERS, 128), 1) % 64
                owner = lax.broadcasted_iota(jnp.int32, (WORKERS, 128), 0)
                hit = (pair == owner) & (lane // WORKERS == c) & (rank == j)
                start = (2 * j + c) * WORKERS
                chosen[start : start + WORKERS, :] = jnp.where(hit, 1.0, 0.0).astype(bf16)

    with jax.named_scope("along_z"):
        pl.semaphore_wait(near, 4)
        for dz in (2, -2):
            tell(line, 0, dz)

    for band in range(4):
        with jax.named_scope("wait_fields"):
            arriving = pl.ds(BAND * band, BAND - ROWS if band == 0 else BAND)
            pltpu.make_async_copy(
                field_all.at[arriving], field_all.at[arriving], field_recv.at[band]
            ).wait()

        with jax.named_scope("phasors"):
            for s in range(BAND * band, BAND * band + BAND, 32):
                field = field_all[s : s + 32, :]
                swapped = pltpu.roll(field, 64, 1)
                lane = lax.broadcasted_iota(jnp.int32, (32, 128), 1)
                low = lane < 64
                slip = jnp.where(low, field, swapped)
                turn = jnp.where(low, swapped, field) * (1.0 / (NT * TIME_STEP))
                first = ((2 * core + place) * QUARTER + jnp.where(low, 0, STEPS)).astype(f32)
                cos0, sin0 = cos_sin_turns(turn * first)
                cos1, sin1 = cos_sin_turns(turn)
                at = s + s // 128 * 128

                def step(k, carry, at=at, cos1=cos1, sin1=sin1):
                    cos, sin = carry
                    phasors[k, at : at + 32, :] = cos.astype(bf16)
                    phasors[k, at + 128 : at + 160, :] = sin.astype(bf16)
                    return cos * cos1 - sin * sin1, sin * cos1 + cos * sin1

                lax.fori_loop(0, STEPS, step, (slip * cos0, slip * sin0), unroll=32)

    with jax.named_scope("along_x"):
        pl.semaphore_wait(line, 2)
        for dx in (1, 2, 3):
            tell(everyone, dx, 0)

    for half in range(2):
        with jax.named_scope("wait_green"):
            arriving = pl.ds(128 * half, 128 - ROWS if half == 0 else 128)
            pltpu.make_async_copy(
                green_all.at[arriving], green_all.at[arriving], green_recv.at[half]
            ).wait()

        with jax.named_scope("green"):
            for c in range(2):
                turned = jnp.transpose(
                    green_all[128 * half : 128 * half + 128, 128 * c : 128 * c + 128]
                )
                for h in range(2):
                    value = [
                        turned[QUARTER * part + STEPS * h : QUARTER * part + STEPS * h + STEPS, :]
                        for part in range(2)
                    ]
                    real = pl.ds(4 * h + 2 * c, STEPS, stride=8)
                    imag = pl.ds(4 * h + 2 * c + 1, STEPS, stride=8)
                    lhs[2 * half, real, :] = value[0]
                    lhs[2 * half, imag, :] = value[1]
                    lhs[2 * half + 1, real, :] = value[1]
                    lhs[2 * half + 1, imag, :] = -value[0]

        with jax.named_scope("spectra"):

            def product(k, _, half=half):
                rows = pl.ds(pl.multiple_of(16 * k, 16), 16)
                depth = slice(256 * half, 256 * half + 256)
                both = jnp.dot(
                    jnp.concatenate([lhs[2 * half + i, rows, :] for i in range(2)], axis=1).astype(
                        bf16
                    ),
                    jnp.concatenate(
                        [phasors[2 * k, depth, :], phasors[2 * k + 1, depth, :]], axis=1
                    ),
                    preferred_element_type=f32,
                )
                value = jnp.concatenate([both[:8, :128], both[8:, 128:]], axis=0)
                spectra[rows, :] = value if half == 0 else spectra[rows, :] + value
                return 0

            lax.fori_loop(0, STEPS // 2, product, 0, unroll=UNROLL)

    contract = (((1,), (1,)), ((), ()))
    with jax.named_scope("place"):
        low = lax.broadcasted_iota(jnp.int32, (STEPS, 128), 1) < 64
        for c in range(2):
            parts = []
            for r in (2 * c, 2 * c + 1):
                parts.append(jnp.where(low, spectra[pl.ds(r, STEPS, stride=8), :], 0.0))
                parts.append(jnp.where(low, 0.0, spectra[pl.ds(4 + r, STEPS, stride=8), :]))
            rest = jnp.concatenate(parts, axis=0)
            value = jnp.zeros((2 * MOST * WORKERS, 128), f32)
            for _ in range(3):
                piece = rest.astype(bf16)
                rest = rest - piece.astype(f32)
                value = value + lax.dot_general(
                    chosen[...], piece, contract, preferred_element_type=f32
                )
            for block in range(2 * MOST):
                partial[pl.ds(2 * WORKERS * block + c, WORKERS, stride=2), :] = value[
                    WORKERS * block : WORKERS * block + WORKERS
                ]

    with jax.named_scope("all_here"):
        pl.semaphore_wait(everyone, 3)

    def part(j, c, w):
        return pl.ds(pl.multiple_of(2 * (WORKERS * (2 * j + c) + w), 2), 2)

    with jax.named_scope("send_sums"):
        for j, to, c in ORDER:
            slot, source = j, partial.at[part(j, c, to)]
            if (j, to, c) == EXTRA:
                aside = jnp.where(row == 0, 1, 0)
                slot, c = j + aside, c - aside
            copy = pltpu.make_async_remote_copy(
                src_ref=source,
                dst_ref=arrived.at[slot, part(0, core, worker)],
                send_sem=sum_send,
                recv_sem=sum_recv.at[slot],
                device_id={"group": 2 * row + c, "worker": to},
                device_id_type=MESH,
            )
            pl.when((worker != to) | (core != c))(copy.start)
        for j in range(MOST):
            arrived[j, part(0, core, worker), :] = partial[part(j, core, worker), :]

        @pl.when(helper)
        def _():
            arrived[MOST, part(0, core, worker), :] = partial[part(MOST - 1, 1, worker), :]

    most = pl.ds(0, 2 * (2 * WORKERS - 1))
    def peaks(j):
        with jax.named_scope("wait_sums"):
            pltpu.make_async_copy(
                arrived.at[j, most], arrived.at[j, most], sum_recv.at[j]
            ).wait()

        with jax.named_scope("weigh"):
            spec = []
            for h in range(2):
                total = arrived[j, 2 * WORKERS * h : 2 * WORKERS * h + 8, :]
                for i in range(8, 2 * WORKERS, 8):
                    total = total + arrived[j, 2 * WORKERS * h + i : 2 * WORKERS * h + i + 8, :]
                spec.append(total[:4] + total[4:])
            real, imag = [], []
            for c in range(2):
                for h in range(2):
                    near_part, far_part = spec[h][c : c + 1], spec[h][2 + c : 3 + c]
                    spec_real = jnp.concatenate([near_part[:, :64], far_part[:, :64]], axis=1)
                    spec_imag = jnp.concatenate([near_part[:, 64:], far_part[:, 64:]], axis=1)
                    gain_real = gain[0, :, 128 * h : 128 * h + 128]
                    gain_imag = gain[1, :, 128 * h : 128 * h + 128]
                    real.append((spec_real * gain_real - spec_imag * gain_imag).astype(bf16))
                    imag.append((spec_real * gain_imag + spec_imag * gain_real).astype(bf16))
            weighted = [
                [jnp.concatenate(v[2 * c : 2 * c + 2], axis=1) for v in (real, imag)]
                for c in range(2)
            ]

        with jax.named_scope("response"):
            tops = []
            for c in range(2):
                best = jnp.zeros((8, NP), f32)
                for start, size in BLOCKS:
                    even, odd = [
                        lax.dot_general(
                            basis[i, start : start + size, :],
                            weighted[c][i],
                            contract,
                            preferred_element_type=f32,
                        )
                        for i in range(2)
                    ]
                    value = jnp.abs(even) + jnp.abs(odd)
                    for t in range(0, size, 8):
                        best = jnp.maximum(best, value[t : t + 8])
                tops.append(jnp.max(best, axis=0, keepdims=True) * (1.0 / math.sqrt(NF)))
        return jnp.concatenate(tops, axis=1)

    give = pltpu.make_async_remote_copy(
        src_ref=given,
        dst_ref=given,
        send_sem=give_send,
        recv_sem=give_recv,
        device_id={"group": 2 * row + 1 - core},
        device_id_type=MESH,
    )

    @pl.when(helper)
    def _():
        given[...] = peaks(MOST)
        give.start()

    for j in range(MOST - 1):
        out_ref[j : j + 1, :] = peaks(j)

    @pl.when(jnp.logical_not(helped))
    def _():
        out_ref[MOST - 1 : MOST, :] = peaks(MOST - 1)

    @pl.when(helped)
    def _():
        give.wait_recv()
        out_ref[MOST - 1 : MOST, :] = given[...]

    with jax.named_scope("wait_sent"):
        others = pl.ds(0, ROWS * (PARTNERS - 1))
        pltpu.make_async_copy(field_all.at[others], field_all.at[others], field_send).wait()
        pltpu.make_async_copy(green_all.at[others], green_all.at[others], green_send).wait()
        for j in range(MOST - 1):
            pltpu.make_async_copy(arrived.at[j, most], arrived.at[j, most], sum_send).wait()
        fewer, one = pl.ds(0, 2 * (2 * WORKERS - 2)), pl.ds(0, 2)
        pltpu.make_async_copy(arrived.at[0, fewer], arrived.at[0, fewer], sum_send).wait()
        last = pltpu.make_async_copy(arrived.at[0, one], arrived.at[0, one], sum_send)
        pl.when(jnp.logical_not(helper))(last.wait)
        pl.when(helped)(last.wait)
        pl.when(helper)(give.wait_send)


def local(green_tensor, slip_field, rupture_time, periods, owner_map):
    vmem = pl.BlockSpec(memory_space=pltpu.VMEM)
    dma = pltpu.SemaphoreType.DMA
    return pl.pallas_call(
        kernel,
        out_shape=jax.ShapeDtypeStruct((MOST, 2 * NP), f32),
        in_specs=[pl.BlockSpec(memory_space=pltpu.HBM)] * 5,
        out_specs=vmem,
        scratch_shapes=[
            pltpu.VMEM((ROWS, 4 * NF), bf16),
            pltpu.VMEM((ROWS, NP), f32),
            pltpu.VMEM((ROWS, NP), f32),
            pltpu.VMEM((1, NP), f32),
            pltpu.VMEM((1, GROUPS * WORKERS), jnp.int32),
            pltpu.VMEM((2, TIMES, NF), bf16),
            pltpu.VMEM((4, ROWS, 4 * QUARTER), f32),
            pltpu.VMEM((GROUPS // 2, ROWS, 128), f32),
            pltpu.VMEM((GATHERED, 4 * QUARTER), f32),
            pltpu.VMEM((GATHERED, 128), f32),
            pltpu.VMEM((STEPS, 2 * GATHERED, 128), bf16),
            pltpu.VMEM((4, 8 * STEPS, 128), f32),
            pltpu.VMEM((8 * STEPS, 128), f32),
            pltpu.VMEM((2 * 2 * MOST * WORKERS, 128), f32),
            pltpu.VMEM((MOST + 1, 2 * 2 * WORKERS, 128), f32),
            pltpu.VMEM((2, NP, NF), f32),
            pltpu.VMEM((2 * MOST * WORKERS, 128), bf16),
            pltpu.VMEM((1, 2 * NP), f32),
        ]
        + [dma((5,)), dma, dma((4,)), dma, dma((2,)), dma, dma((MOST + 1,)), dma, dma]
        + [pltpu.SemaphoreType.REGULAR] * 3,
        compiler_params=pltpu.CompilerParams(
            collective_id=0, has_side_effects=True, vmem_limit_bytes=32 * 1024 * 1024
        ),
        name="seismogram",
    )(
        *(
            pltpu.with_memory_space_constraint(x, pltpu.HBM)
            for x in (
                green_tensor,
                slip_field,
                rupture_time,
                periods.reshape(1, NP),
                owner_map.reshape(1, -1),
            )
        )
    )


def solution(mesh):
    placed = (
        P(("group", "worker"), None),
        P(("group", "worker"), None),
        P(("group", "worker"), None),
        P(),
        P(),
    )
    return jax.shard_map(
        local, mesh=mesh, in_specs=placed, out_specs=P(("group", "worker"), None), check_vma=False
    )
```

```python
import functools
import math

import jax
import jax.numpy as jnp
from jax import lax
from jax.experimental import pallas as pl
from jax.experimental.pallas import tpu as pltpu
from jax.sharding import PartitionSpec as P

NT = 4096
NF = 256
NP = 256
MOST = 3
TIME_STEP = 0.05
DAMPING = 0.05

GROUPS = 8
WORKERS = 32
LINE = 8
ROWS = 16
EXTRA = (MOST - 1, 0, 1)
ORDER = [
    (j, x * LINE + z, c)
    for j in range(MOST)
    for z in (0, 1, 2, 3, 7, 6, 5, 4)
    for x in (0, 1, 3, 2)
    for c in (1, 0)
]
ORDER.remove(EXTRA)
ORDER.insert(1, EXTRA)
SENDS = [(to, 0) for to in (0, 1, 2, 3, 12, 13, 14, 15, 8, 9, 10, 11, 4, 5, 6, 7)] + [
    (to, 1) for to in (0, 1, 2, 3, 12, 13, 14, 15, 8, 9, 10, 11, 4, 5, 6, 7)
]
PARTNERS = 16
GATHERED = ROWS * PARTNERS
BAND = 64
UNROLL = 16
QUARTER = 64
STEPS = 32
TIMES = NT // 2 + 16
BLOCKS = [(0, 512), (512, 512), (1024, 512), (1536, 528)]

f32 = jnp.float32
bf16 = jnp.bfloat16
MESH = pl.DeviceIdType.MESH


def cos_sin_turns(turns):
    near = turns - jnp.round(turns)
    angle = near * (2.0 * math.pi)
    square = angle * angle
    cos = f32(0.0)
    for n in range(8, -1, -1):
        cos = cos * square + f32((-1) ** n / math.factorial(2 * n))
    sin = f32(0.0)
    for n in range(8, -1, -1):
        sin = sin * square + f32((-1) ** n / math.factorial(2 * n + 1))
    return cos, sin * angle


def kernel(
    green_hbm, slip_hbm, time_hbm, periods_hbm, owner_hbm, out_ref,
    green_ref, slip_ref, time_ref, periods_ref, owner_ref, basis, green_stage, field_stage, green_all, field_all, phasors, lhs, spectra,
    partial, arrived, gain, chosen, given,
    load_sem, field_send, field_recv, green_send, green_recv,
    sum_send, sum_recv, give_send, give_recv,
    near, line, everyone,
):
    group = lax.axis_index("group")
    worker = lax.axis_index("worker")
    row, core = group // 2, group % 2

    x, z = worker // LINE, worker % LINE

    def tell(semaphore, dx, dz):
        to = (x + dx) % (WORKERS // LINE) * LINE + (z + dz) % LINE
        pl.semaphore_signal(semaphore, inc=1, device_id={"worker": to}, device_id_type=MESH)

    place = z % 2
    helped = (row == 0) & (worker == 0) & (core == 1)
    helper = (row == 0) & (worker == 0) & (core == 0)
    me = 2 * group + place

    def partner(i):
        return {"group": i // 2, "worker": worker - place + i % 2}

    barrier = pltpu.get_barrier_semaphore()
    for i in range(1, PARTNERS):
        pl.semaphore_signal(
            barrier, inc=1, device_id=partner((me + i) % PARTNERS), device_id_type=MESH
        )
    loads = [
        pltpu.make_async_copy(source, target, load_sem.at[i])
        for i, (source, target) in enumerate(
            [
                (slip_hbm, slip_ref),
                (time_hbm, time_ref),
                (green_hbm, green_ref),
                (periods_hbm, periods_ref),
                (owner_hbm, owner_ref),
            ]
        )
    ]
    for load in loads:
        load.start()
    for dx, dz in ((0, 1), (0, -1), (1, 0), (-1, 0)):
        tell(barrier, dx, dz)

    for load in loads[:3]:
        load.wait()
    with jax.named_scope("stage"):
        for y in range(GROUPS // 2):
            lanes = slice(64 * y, 64 * y + 64)
            field_stage[y] = jnp.concatenate([slip_ref[:, lanes], time_ref[:, lanes]], axis=1)
        for part in range(4):
            for quarter in range(4):
                start = part * NF + quarter * QUARTER
                green_stage[quarter, :, part * QUARTER : (part + 1) * QUARTER] = green_ref[
                    :, start : start + QUARTER
                ].astype(f32)

    with jax.named_scope("barrier"):
        pl.semaphore_wait(barrier, PARTNERS - 1 + 4)

    own = pl.ds(pl.multiple_of(ROWS * (2 * core + place), ROWS), ROWS)

    def spot(to):
        away = (row - to // 4 + 4) % 4
        return away + away // 2 * (5 - 2 * away)

    def send(to, which):
        rows = pl.ds(pl.multiple_of(BAND * spot(to) + ROWS * (2 * core + place), ROWS), ROWS)
        if which == 0:
            source, target = field_stage.at[to // 4], field_all.at[rows]
            sent, received = field_send, field_recv.at[spot(to)]
        else:
            source, target = green_stage.at[to % 4], green_all.at[rows]
            sent, received = green_send, green_recv.at[spot(to) // 2]
        pltpu.make_async_remote_copy(
            src_ref=source,
            dst_ref=target,
            send_sem=sent,
            recv_sem=received,
            device_id=partner(to),
            device_id_type=MESH,
        ).start()

    with jax.named_scope("send_inputs"):
        for dx, dz in ((0, 1), (0, -1), (1, 0), (-1, 0)):
            tell(near, dx, dz)
        for to, which in SENDS:
            pl.when(me != to)(functools.partial(send, to, which))
    field_all[own, :] = field_stage[row]
    green_all[own, :] = green_stage[2 * core + place]

    for load in loads[3:]:
        load.wait()
    with jax.named_scope("gain"):
        natural = (2.0 * math.pi) / periods_ref[...]
        column = jnp.concatenate(
            [
                jnp.transpose(jnp.broadcast_to(natural[:, :128], (128, 128))),
                jnp.transpose(jnp.broadcast_to(natural[:, 128:], (128, 128))),
            ],
            axis=0,
        )
        for h in range(2):
            index = lax.broadcasted_iota(jnp.int32, (NP, 128), 1) + 128 * h
            angular = (2.0 * math.pi) * index.astype(f32) / (NT * TIME_STEP)
            denom_real = column * column - angular * angular
            denom_imag = (2.0 * DAMPING) * column * angular
            scale = column * column / (denom_real * denom_real + denom_imag * denom_imag)
            gain[0, :, 128 * h : 128 * h + 128] = -scale * denom_real
            gain[1, :, 128 * h : 128 * h + 128] = scale * denom_imag

    with jax.named_scope("basis"):
        freq = lax.broadcasted_iota(jnp.int32, (16, NF), 1)
        time = lax.broadcasted_iota(jnp.int32, (16, NF), 0)
        fold = jnp.where(freq == 0, 1.0, 2.0)
        cos0, sin0 = cos_sin_turns((freq * time).astype(f32) * (1.0 / NT))
        cos16, sin16 = cos_sin_turns(freq.astype(f32) * (16.0 / NT))

        def advance(b, carry):
            cos, sin = carry
            rows = pl.ds(pl.multiple_of(16 * b, 16), 16)
            basis[0, rows, :] = cos.astype(bf16)
            basis[1, rows, :] = sin.astype(bf16)
            return cos * cos16 + sin * sin16, sin * cos16 - cos * sin16

        lax.fori_loop(0, TIMES // 16, advance, (fold * cos0, -fold * sin0), unroll=3)

    with jax.named_scope("owners"):
        pair = owner_ref[:, 0:64]
        for y in range(1, GROUPS // 2):
            pair = jnp.where(row == y, owner_ref[:, 64 * y : 64 * y + 64], pair)
        pair = jnp.concatenate([pair, pair], axis=1)
        lane = lax.broadcasted_iota(jnp.int32, (128, 128), 1) % 64
        other = lax.broadcasted_iota(jnp.int32, (128, 128), 0)
        named = jnp.broadcast_to(pair, (128, 128))
        same = (jnp.transpose(named) == named) & (other // WORKERS == lane // WORKERS)
        earlier = jnp.where(same & (other < lane), 1.0, 0.0)
        rank = jnp.sum(earlier, axis=0, keepdims=True).astype(jnp.int32)
        for j in range(MOST):
            for c in range(2):
                lane = lax.broadcasted_iota(jnp.int32, (WORKERS, 128), 1) % 64
                owner = lax.broadcasted_iota(jnp.int32, (WORKERS, 128), 0)
                hit = (pair == owner) & (lane // WORKERS == c) & (rank == j)
                start = (2 * j + c) * WORKERS
                chosen[start : start + WORKERS, :] = jnp.where(hit, 1.0, 0.0).astype(bf16)

    with jax.named_scope("along_z"):
        pl.semaphore_wait(near, 4)
        for dz in (2, -2):
            tell(line, 0, dz)

    for band in range(4):
        if band == 1:
            with jax.named_scope("along_x"):
                pl.semaphore_wait(line, 2)
                for dx in (1, 2, 3):
                    tell(everyone, dx, 0)

        with jax.named_scope("wait_fields"):
            arriving = pl.ds(BAND * band, BAND - ROWS if band == 0 else BAND)
            pltpu.make_async_copy(
                field_all.at[arriving], field_all.at[arriving], field_recv.at[band]
            ).wait()

        with jax.named_scope("phasors"):
            for s in range(BAND * band, BAND * band + BAND, 32):
                field = field_all[s : s + 32, :]
                swapped = pltpu.roll(field, 64, 1)
                lane = lax.broadcasted_iota(jnp.int32, (32, 128), 1)
                low = lane < 64
                slip = jnp.where(low, field, swapped)
                turn = jnp.where(low, swapped, field) * (1.0 / (NT * TIME_STEP))
                first = ((2 * core + place) * QUARTER + jnp.where(low, 0, STEPS)).astype(f32)
                cos0, sin0 = cos_sin_turns(turn * first)
                cos1, sin1 = cos_sin_turns(turn)
                at = s + s // 128 * 128

                def step(k, carry, at=at, cos1=cos1, sin1=sin1):
                    cos, sin = carry
                    phasors[k, at : at + 32, :] = cos.astype(bf16)
                    phasors[k, at + 128 : at + 160, :] = sin.astype(bf16)
                    return cos * cos1 - sin * sin1, sin * cos1 + cos * sin1

                lax.fori_loop(0, STEPS, step, (slip * cos0, slip * sin0), unroll=32)

    for half in range(2):
        with jax.named_scope("wait_green"):
            arriving = pl.ds(128 * half, 128 - ROWS if half == 0 else 128)
            pltpu.make_async_copy(
                green_all.at[arriving], green_all.at[arriving], green_recv.at[half]
            ).wait()

        with jax.named_scope("green"):
            for c in range(2):
                turned = jnp.transpose(
                    green_all[128 * half : 128 * half + 128, 128 * c : 128 * c + 128]
                )
                for h in range(2):
                    value = [
                        turned[QUARTER * part + STEPS * h : QUARTER * part + STEPS * h + STEPS, :]
                        for part in range(2)
                    ]
                    real = pl.ds(4 * h + 2 * c, STEPS, stride=8)
                    imag = pl.ds(4 * h + 2 * c + 1, STEPS, stride=8)
                    lhs[2 * half, real, :] = value[0]
                    lhs[2 * half, imag, :] = value[1]
                    lhs[2 * half + 1, real, :] = value[1]
                    lhs[2 * half + 1, imag, :] = -value[0]

        with jax.named_scope("spectra"):

            def product(k, _, half=half):
                rows = pl.ds(pl.multiple_of(16 * k, 16), 16)
                depth = slice(256 * half, 256 * half + 256)
                both = jnp.dot(
                    jnp.concatenate([lhs[2 * half + i, rows, :] for i in range(2)], axis=1).astype(
                        bf16
                    ),
                    jnp.concatenate(
                        [phasors[2 * k, depth, :], phasors[2 * k + 1, depth, :]], axis=1
                    ),
                    preferred_element_type=f32,
                )
                value = jnp.concatenate([both[:8, :128], both[8:, 128:]], axis=0)
                spectra[rows, :] = value if half == 0 else spectra[rows, :] + value
                return 0

            lax.fori_loop(0, STEPS // 2, product, 0, unroll=UNROLL)

    contract = (((1,), (1,)), ((), ()))
    with jax.named_scope("place"):
        low = lax.broadcasted_iota(jnp.int32, (STEPS, 128), 1) < 64
        for c in range(2):
            parts = []
            for r in (2 * c, 2 * c + 1):
                parts.append(jnp.where(low, spectra[pl.ds(r, STEPS, stride=8), :], 0.0))
                parts.append(jnp.where(low, 0.0, spectra[pl.ds(4 + r, STEPS, stride=8), :]))
            rest = jnp.concatenate(parts, axis=0)
            value = jnp.zeros((2 * MOST * WORKERS, 128), f32)
            for _ in range(3):
                piece = rest.astype(bf16)
                rest = rest - piece.astype(f32)
                value = value + lax.dot_general(
                    chosen[...], piece, contract, preferred_element_type=f32
                )
            for block in range(2 * MOST):
                partial[pl.ds(2 * WORKERS * block + c, WORKERS, stride=2), :] = value[
                    WORKERS * block : WORKERS * block + WORKERS
                ]

    with jax.named_scope("all_here"):
        pl.semaphore_wait(everyone, 3)

    def part(j, c, w):
        return pl.ds(pl.multiple_of(2 * (WORKERS * (2 * j + c) + w), 2), 2)

    with jax.named_scope("send_sums"):
        for j, to, c in ORDER:
            slot, source = j, partial.at[part(j, c, to)]
            if (j, to, c) == EXTRA:
                aside = jnp.where(row == 0, 1, 0)
                slot, c = j + aside, c - aside
            copy = pltpu.make_async_remote_copy(
                src_ref=source,
                dst_ref=arrived.at[slot, part(0, core, worker)],
                send_sem=sum_send,
                recv_sem=sum_recv.at[slot],
                device_id={"group": 2 * row + c, "worker": to},
                device_id_type=MESH,
            )
            pl.when((worker != to) | (core != c))(copy.start)
        for j in range(MOST):
            arrived[j, part(0, core, worker), :] = partial[part(j, core, worker), :]

        @pl.when(helper)
        def _():
            arrived[MOST, part(0, core, worker), :] = partial[part(MOST - 1, 1, worker), :]

    most = pl.ds(0, 2 * (2 * WORKERS - 1))
    def peaks(j):
        with jax.named_scope("wait_sums"):
            pltpu.make_async_copy(
                arrived.at[j, most], arrived.at[j, most], sum_recv.at[j]
            ).wait()

        with jax.named_scope("weigh"):
            spec = []
            for h in range(2):
                total = arrived[j, 2 * WORKERS * h : 2 * WORKERS * h + 8, :]
                for i in range(8, 2 * WORKERS, 8):
                    total = total + arrived[j, 2 * WORKERS * h + i : 2 * WORKERS * h + i + 8, :]
                spec.append(total[:4] + total[4:])
            real, imag = [], []
            for c in range(2):
                for h in range(2):
                    near_part, far_part = spec[h][c : c + 1], spec[h][2 + c : 3 + c]
                    spec_real = jnp.concatenate([near_part[:, :64], far_part[:, :64]], axis=1)
                    spec_imag = jnp.concatenate([near_part[:, 64:], far_part[:, 64:]], axis=1)
                    gain_real = gain[0, :, 128 * h : 128 * h + 128]
                    gain_imag = gain[1, :, 128 * h : 128 * h + 128]
                    real.append((spec_real * gain_real - spec_imag * gain_imag).astype(bf16))
                    imag.append((spec_real * gain_imag + spec_imag * gain_real).astype(bf16))
            weighted = [
                [jnp.concatenate(v[2 * c : 2 * c + 2], axis=1) for v in (real, imag)]
                for c in range(2)
            ]

        with jax.named_scope("response"):
            tops = []
            for c in range(2):
                best = jnp.zeros((8, NP), f32)
                for start, size in BLOCKS:
                    even, odd = [
                        lax.dot_general(
                            basis[i, start : start + size, :],
                            weighted[c][i],
                            contract,
                            preferred_element_type=f32,
                        )
                        for i in range(2)
                    ]
                    value = jnp.abs(even) + jnp.abs(odd)
                    for t in range(0, size, 8):
                        best = jnp.maximum(best, value[t : t + 8])
                tops.append(jnp.max(best, axis=0, keepdims=True) * (1.0 / math.sqrt(NF)))
        return jnp.concatenate(tops, axis=1)

    give = pltpu.make_async_remote_copy(
        src_ref=given,
        dst_ref=given,
        send_sem=give_send,
        recv_sem=give_recv,
        device_id={"group": 2 * row + 1 - core},
        device_id_type=MESH,
    )

    @pl.when(helper)
    def _():
        given[...] = peaks(MOST)
        give.start()

    for j in range(MOST - 1):
        out_ref[j : j + 1, :] = peaks(j)

    @pl.when(jnp.logical_not(helped))
    def _():
        out_ref[MOST - 1 : MOST, :] = peaks(MOST - 1)

    @pl.when(helped)
    def _():
        give.wait_recv()
        out_ref[MOST - 1 : MOST, :] = given[...]

    with jax.named_scope("wait_sent"):
        others = pl.ds(0, ROWS * (PARTNERS - 1))
        pltpu.make_async_copy(field_all.at[others], field_all.at[others], field_send).wait()
        pltpu.make_async_copy(green_all.at[others], green_all.at[others], green_send).wait()
        for j in range(MOST - 1):
            pltpu.make_async_copy(arrived.at[j, most], arrived.at[j, most], sum_send).wait()
        fewer, one = pl.ds(0, 2 * (2 * WORKERS - 2)), pl.ds(0, 2)
        pltpu.make_async_copy(arrived.at[0, fewer], arrived.at[0, fewer], sum_send).wait()
        last = pltpu.make_async_copy(arrived.at[0, one], arrived.at[0, one], sum_send)
        pl.when(jnp.logical_not(helper))(last.wait)
        pl.when(helped)(last.wait)
        pl.when(helper)(give.wait_send)


def local(green_tensor, slip_field, rupture_time, periods, owner_map):
    vmem = pl.BlockSpec(memory_space=pltpu.VMEM)
    dma = pltpu.SemaphoreType.DMA
    return pl.pallas_call(
        kernel,
        out_shape=jax.ShapeDtypeStruct((MOST, 2 * NP), f32),
        in_specs=[pl.BlockSpec(memory_space=pltpu.HBM)] * 5,
        out_specs=vmem,
        scratch_shapes=[
            pltpu.VMEM((ROWS, 4 * NF), bf16),
            pltpu.VMEM((ROWS, NP), f32),
            pltpu.VMEM((ROWS, NP), f32),
            pltpu.VMEM((1, NP), f32),
            pltpu.VMEM((1, GROUPS * WORKERS), jnp.int32),
            pltpu.VMEM((2, TIMES, NF), bf16),
            pltpu.VMEM((4, ROWS, 4 * QUARTER), f32),
            pltpu.VMEM((GROUPS // 2, ROWS, 128), f32),
            pltpu.VMEM((GATHERED, 4 * QUARTER), f32),
            pltpu.VMEM((GATHERED, 128), f32),
            pltpu.VMEM((STEPS, 2 * GATHERED, 128), bf16),
            pltpu.VMEM((4, 8 * STEPS, 128), f32),
            pltpu.VMEM((8 * STEPS, 128), f32),
            pltpu.VMEM((2 * 2 * MOST * WORKERS, 128), f32),
            pltpu.VMEM((MOST + 1, 2 * 2 * WORKERS, 128), f32),
            pltpu.VMEM((2, NP, NF), f32),
            pltpu.VMEM((2 * MOST * WORKERS, 128), bf16),
            pltpu.VMEM((1, 2 * NP), f32),
        ]
        + [dma((5,)), dma, dma((4,)), dma, dma((2,)), dma, dma((MOST + 1,)), dma, dma]
        + [pltpu.SemaphoreType.REGULAR] * 3,
        compiler_params=pltpu.CompilerParams(
            collective_id=0, has_side_effects=True, vmem_limit_bytes=32 * 1024 * 1024
        ),
        name="seismogram",
    )(
        *(
            pltpu.with_memory_space_constraint(x, pltpu.HBM)
            for x in (
                green_tensor,
                slip_field,
                rupture_time,
                periods.reshape(1, NP),
                owner_map.reshape(1, -1),
            )
        )
    )


def solution(mesh):
    placed = (
        P(("group", "worker"), None),
        P(("group", "worker"), None),
        P(("group", "worker"), None),
        P(),
        P(),
    )
    return jax.shard_map(
        local, mesh=mesh, in_specs=placed, out_specs=P(("group", "worker"), None), check_vma=False
    )
```
